256 devices in a mesh: seq: 32 (over y_lo, z, core), exp: 8 (over y_hi, x).
Axes of the slice: x: 4, y: 4 (y_hi: 2, y_lo: 2; y = y_hi * 2 + y_lo), z: 8, core: 2. Of those that a mesh axis runs over, the one named last changes fastest.
Arguments:
- tokens: bfloat16 [3, 65536, 1280], P(None, ('seq', 'exp')), may hold values from -64 to 64
- router: bfloat16 [1280, 128], replicated, may hold values from -1 to 1
- w_in: bfloat16 [64, 1280, 5120], P('seq', None, 'exp'), may hold values from -0.15625 to 0.15625
- w_out: bfloat16 [64, 5120, 1280], P('seq', 'exp'), may hold values from -0.078125 to 0.078125
- cotangent: bfloat16 [3, 65536, 1280], P(None, ('seq', 'exp')), may hold values from -6 to 6
Outputs:
- d_tokens: bfloat16 [3, 65536, 1280], P(None, ('seq', 'exp'))
- d_router: float32 [1280, 128], replicated
The draws below stay inside these ranges and needn't reach their ends.
All inputs are finite; a program needn't handle non-finite values.
Results may differ from the reference program's by a relative error of at most 0.02.
Values may be sent and summed in bfloat16 or wider, within the bound.
No kernel may reach another device: no remote copies, remote signals or barrier semaphores. Data moves between devices by JAX's collectives and lax.ppermute only.
A program may use at most 64 MiB of HBM per device.

```python
import math
import jax
import jax.numpy as jnp
from jax import lax

D = 1280
HID = 5120
SPE = 2
CLIPS = 3
EXPERTS = 64
SLOTS = 128
LEN = 65536


def shared_router(key):
    values = jax.random.normal(jax.random.fold_in(key, 101), (D, SLOTS), jnp.float32)
    return jnp.clip(values * (3.0 / math.sqrt(D)), -1.0, 1.0)


def draw_router(key, part):
    return shared_router(key).astype(jnp.bfloat16)


def draw_tokens(key, part):
    key = jax.random.fold_in(key, 3)
    subkeys = jax.random.split(key, 1)
    values = jax.random.normal(subkeys[0], (CLIPS, LEN, D), jnp.float32)
    return jnp.clip(values, -64.0, 64.0).astype(jnp.bfloat16)


def steps_of(own_key, extent, shards, smallest, largest):
    def one(position, shards_of):
        draws = jax.random.uniform(jax.random.fold_in(jax.random.fold_in(own_key, 6), position), (shards_of,), jnp.float32, smallest / len(shards), largest / len(shards))
        return jnp.repeat(jnp.exp(draws), extent[position] // shards_of).reshape((-1,) + (1,) * (len(extent) - position - 1))

    loudness = one(*shards[0])
    for cut in shards[1:]:
        loudness = loudness * one(*cut)
    return loudness


def normal_values(own_key, shape, spread, bound, cuts=(), kind=jnp.bfloat16):
    level = steps_of(own_key, shape, cuts, -0.22, 0.18) if cuts else 1.0
    array = jax.random.normal(own_key, shape, jnp.float32) * spread * level
    return jnp.minimum(jnp.maximum(array, -bound), bound).astype(kind)


def setup_inputs(seed: int = 0) -> dict:
    seeds = jax.random.split(jax.random.key(seed), 6)
    tokens = draw_tokens(jax.random.fold_in(seeds[5], 71), 0)
    router = draw_router(jax.random.fold_in(seeds[5], 71), 0)
    w_in = normal_values(seeds[2], (EXPERTS, D, HID), D ** -0.5, 0.15625, ((0, 32), (2, 8)))
    w_out = normal_values(seeds[3], (EXPERTS, HID, D), HID ** -0.5, 0.078125, ((0, 32), (1, 8)))
    cotangent = normal_values(seeds[4], (CLIPS, LEN, D), 1.0, 6.0, ((1, 256),))
    return {"tokens": tokens, "router": router, "w_in": w_in, "w_out": w_out, "cotangent": cotangent}


def gelu_tanh(values):
    return jax.nn.gelu(values, approximate=True)

def column_softmax(logits):
    peak = lax.optimization_barrier(jnp.max(logits, axis=0, keepdims=True))
    raised = jnp.exp(logits - peak)
    return raised / lax.optimization_barrier(jnp.sum(raised, axis=0, keepdims=True))

def row_softmax(logits):
    peak = lax.optimization_barrier(jnp.max(logits, axis=1, keepdims=True))
    raised = jnp.exp(logits - peak)
    return raised / lax.optimization_barrier(jnp.sum(raised, axis=1, keepdims=True))

def by_expert(slots):
    return slots.reshape(CLIPS, EXPERTS, SPE, D).transpose(1, 0, 2, 3).reshape(EXPERTS, CLIPS * SPE, D)

def by_clip(rows):
    return rows.reshape(EXPERTS, CLIPS, SPE, D).transpose(1, 0, 2, 3).reshape(CLIPS, SLOTS, D)

def reference(tokens, router, w_in, w_out, cotangent):

    def forward_clip(tokens_clip):
        logits = jnp.dot(tokens_clip, router, preferred_element_type=jnp.float32)
        dispatch_low = column_softmax(logits).astype(jnp.bfloat16)
        return jnp.dot(dispatch_low.T, tokens_clip, preferred_element_type=jnp.float32).astype(jnp.bfloat16)
    slot_in = lax.map(forward_clip, tokens)

    def expert_apply(items):
        rows, first, second = items
        preact = jnp.dot(rows, first, preferred_element_type=jnp.float32)
        hidden = gelu_tanh(preact).astype(jnp.bfloat16)
        return jnp.dot(hidden, second, preferred_element_type=jnp.float32).astype(jnp.bfloat16)
    slot_out = by_clip(lax.map(expert_apply, (by_expert(slot_in), w_in, w_out)))

    def combine_clip(items):
        tokens_clip, cot_clip = items
        logits = jnp.dot(tokens_clip, router, preferred_element_type=jnp.float32)
        combine_low = row_softmax(logits).astype(jnp.bfloat16)
        return jnp.dot(combine_low.T, cot_clip, preferred_element_type=jnp.float32).astype(jnp.bfloat16)
    d_slot_out = lax.map(combine_clip, (tokens, cotangent))

    def expert_back(items):
        rows, grads, first, second = items
        preact = jnp.dot(rows, first, preferred_element_type=jnp.float32)
        d_hidden = jnp.dot(grads, second.T, preferred_element_type=jnp.float32)
        d_preact = jax.vjp(gelu_tanh, preact)[1](d_hidden)[0].astype(jnp.bfloat16)
        return jnp.dot(d_preact, first.T, preferred_element_type=jnp.float32).astype(jnp.bfloat16)
    d_slot_in = by_clip(lax.map(expert_back, (by_expert(slot_in), by_expert(d_slot_out), w_in, w_out)))

    def final_clip(items):
        tokens_clip, cot_clip, out_clip, din_clip = items
        logits = jnp.dot(tokens_clip, router, preferred_element_type=jnp.float32)
        dispatch = column_softmax(logits)
        combine = row_softmax(logits)
        d_combine = jnp.dot(cot_clip, out_clip.T, preferred_element_type=jnp.float32)
        d_logit_c = combine * (d_combine - lax.optimization_barrier(jnp.sum(combine * d_combine, axis=1, keepdims=True)))
        dispatch_low = dispatch.astype(jnp.bfloat16)
        d_via_slots = jnp.dot(dispatch_low, din_clip, preferred_element_type=jnp.float32)
        d_dispatch = jnp.dot(tokens_clip, din_clip.T, preferred_element_type=jnp.float32)
        column_dot = lax.optimization_barrier(jnp.sum(dispatch * d_dispatch, axis=0, keepdims=True))
        d_logit = (d_logit_c + dispatch * (d_dispatch - column_dot)).astype(jnp.bfloat16)
        d_tok = (d_via_slots + jnp.dot(d_logit, router.T, preferred_element_type=jnp.float32)).astype(jnp.bfloat16)
        d_rout = jnp.dot(tokens_clip.T, d_logit, preferred_element_type=jnp.float32)
        return (d_tok, d_rout)
    d_tokens, router_parts = lax.map(final_clip, (tokens, cotangent, slot_out, d_slot_in))
    return (d_tokens, lax.optimization_barrier(jnp.sum(router_parts, axis=0)))
```

```python
import functools

import jax
import jax.numpy as jnp
from jax import lax
from jax.experimental import pallas as pl
from jax.experimental.pallas import tpu as pltpu
from jax.sharding import Mesh, PartitionSpec as P

SIZES = {"yl": 2, "z": 8, "core": 2, "yh": 2, "x": 4}
AXES = tuple(SIZES)
OWNERS = ("yl", "z")
EXP = ("yh", "x")
PLANE = ("yl", "yh", "x")

D = 1280
WIDE = 1408
CLIPS = 3
TOK = 256
ROWS = 24
VMEM = 48 * 1024 * 1024
GELU_C = 0.7978845608028654
GELU_A = 0.044715

bf16 = jnp.bfloat16
f32 = jnp.float32

NT = (((1,), (1,)), ((), ()))
TN = (((0,), (0,)), ((), ()))


def dot(a, b, dims=None):
    if dims is None:
        return jnp.dot(a, b, preferred_element_type=f32)
    return lax.dot_general(a, b, dims, preferred_element_type=f32)


def is_grad_row(shape):
    return lax.broadcasted_iota(jnp.int32, shape, 0) % 8 >= 4


def swap_halves(v, grad):
    n = v.shape[0]
    return jnp.where(grad, pltpu.roll(v, 4, 0), pltpu.roll(v, n - 4, 0))


def pack_stats(columns):
    rows = columns[0].shape[0]
    lane = lax.broadcasted_iota(jnp.int32, (rows, 128), 1)
    out = jnp.zeros((rows, 128), f32)
    for i, value in enumerate(columns):
        high = value.astype(bf16).astype(f32)
        rest = value - high
        middle = rest.astype(bf16).astype(f32)
        for j, part in enumerate((high, middle, rest - middle)):
            out = jnp.where(lane == 3 * i + j, part, out)
    return out


def read_stat(stats, i):
    lane = lax.broadcasted_iota(jnp.int32, stats.shape, 1)
    kept = jnp.where((lane >= 3 * i) & (lane < 3 * i + 3), stats, 0.0)
    return jnp.sum(kept, axis=1, keepdims=True)


def merge(blocks):
    wide = [b.astype(f32) for b in blocks]
    peaks = [read_stat(b[:, D:], 0) for b in wide]
    sums = [read_stat(b[:, D:], 1) for b in wide]
    peak = functools.reduce(jnp.maximum, peaks)
    values = jnp.zeros((wide[0].shape[0], D), f32)
    total = jnp.zeros_like(peak)
    for b, p, s in zip(wide, peaks, sums):
        scale = jnp.exp(p - peak)
        values = values + scale * b[:, :D]
        total = total + scale * s
    return values, peak, total


def call(body, outs, *args, scratch=(), flops=0, nbytes=0, smem=()):
    specs = [
        pl.BlockSpec(memory_space=pltpu.SMEM if i in smem else pltpu.VMEM) for i in range(len(args))
    ]
    return pl.pallas_call(
        body,
        out_shape=[jax.ShapeDtypeStruct(s, t) for s, t in outs],
        in_specs=specs,
        out_specs=[pl.BlockSpec(memory_space=pltpu.VMEM) for _ in outs],
        scratch_shapes=list(scratch),
        compiler_params=pltpu.CompilerParams(vmem_limit_bytes=VMEM),
        cost_estimate=pl.CostEstimate(flops=flops, bytes_accessed=nbytes, transcendentals=0),
    )(*args)


def slots_body(core_ref, tokens, router, cot, mine, theirs, rt_ref, lt_ref, weights_in, weights_out):
    t = lax.broadcasted_iota(jnp.int32, (256, 128), 0)
    s = lax.broadcasted_iota(jnp.int32, (256, 128), 1)
    half = t // 128
    owner_core = half + core_ref[0] * (1 - 2 * half)
    slot = 8 * ((t % 128) // 8) + 4 * owner_core + t % 4
    pick = (s == slot).astype(f32).astype(bf16)
    rt_ref[...] = dot(pick, router[...], NT).astype(bf16)
    grad = is_grad_row((256, TOK))
    grad_col = is_grad_row((256, 1))
    stats = []
    for c in range(CLIPS):
        logits = dot(rt_ref[...], tokens[c], NT)
        lt_ref[c] = logits
        peak = jnp.max(logits, axis=1, keepdims=True)
        low = jnp.where(grad, 0.0, jnp.exp(logits - peak)).astype(bf16)
        total = jnp.sum(low.astype(f32), axis=1, keepdims=True)
        weights_in[c] = low
        raised = jnp.exp(logits - jnp.max(logits, axis=0, keepdims=True))
        combine = raised / (0.5 * jnp.sum(raised, axis=0, keepdims=True))
        weights_out[c] = jnp.where(grad, combine, 0.0).astype(bf16)
        peak = jnp.where(grad_col, 0.0, peak)
        total = jnp.where(grad_col, 1.0, total)
        stats.append(pack_stats([peak, total]).reshape(32, 8, 128))
    packed = jnp.concatenate(stats, axis=1).astype(bf16)
    mine[:, :, D:] = packed[:16]
    theirs[:, :, D:] = packed[16:]

    def chunk(j, carry):
        lanes = pl.ds(pl.multiple_of(j * 256, 256), 256)
        parts = []
        for c in range(CLIPS):
            part = dot(weights_in[c], tokens[c, :, lanes]) + dot(weights_out[c], cot[c, :, lanes])
            parts.append(part.reshape(32, 8, 256))
        full = jnp.concatenate(parts, axis=1).astype(bf16)
        mine[:, :, lanes] = full[:16]
        theirs[:, :, lanes] = full[16:]
        return carry

    lax.fori_loop(0, D // 256, chunk, 0)


def pair_body(a_ref, b_ref, out):
    for d in range(16):
        values, peak, total = merge([a_ref[d], b_ref[d]])
        out[d, :, :D] = values.astype(bf16)
        out[d, :, D:] = pack_stats([peak, total]).astype(bf16)


def owner_body(x_ref, out):
    values, peak, total = merge([x_ref[d] for d in range(16)])
    values = values.astype(bf16)
    stats = pack_stats([peak, total]).astype(bf16)
    for e in range(8):
        out[e, :, :D] = values
        out[e, :, D:] = stats


def gelu_parts(v):
    t = jnp.tanh(GELU_C * (v + GELU_A * (v * v * v)))
    value = 0.5 * v * (1.0 + t)
    slope = 0.5 * (1.0 + t) + 0.5 * v * (1.0 - t * t) * (GELU_C * (1.0 + 3.0 * GELU_A * (v * v)))
    return value, slope


def expert_body(x_ref, w_in, w_out, out, keep):
    values, peak, total = merge([x_ref[e] for e in range(8)])
    grad_col = is_grad_row((ROWS, 1))
    rows = values * jnp.where(grad_col, 1.0, 1.0 / total)
    keep[:, :D] = rows
    keep[:, D:] = pack_stats([peak, total])
    low = rows.astype(bf16)
    row = lax.broadcasted_iota(jnp.int32, (ROWS, 640), 0)
    grad = row % 8 >= 4
    acc = jnp.zeros((ROWS, D), f32)
    for i in range(2):
        own = (row % 4) // 2 == i
        value, slope = gelu_parts(dot(low, w_in[i]))
        d_pre = dot(low, w_out[i], NT) * pltpu.roll(slope, 4, 0)
        hidden = jnp.where(own & jnp.logical_not(grad), value, 0.0).astype(bf16)
        d_pre = jnp.where(own & grad, d_pre, 0.0).astype(bf16)
        acc = acc + dot(hidden, w_out[i]) + dot(d_pre, w_in[i], NT)
    acc = acc.astype(bf16)
    for e in range(8):
        out[e] = acc


def result_body(x_ref, keep, out):
    acc = x_ref[0].astype(f32)
    for e in range(1, 8):
        acc = acc + x_ref[e].astype(f32)
    low = acc.astype(bf16)
    slot_in = keep[:, :D]
    column_dot = jnp.sum(low.astype(f32) * pltpu.roll(slot_in, 4, 0), axis=1, keepdims=True)
    peak = read_stat(keep[:, D:], 0)
    total = read_stat(keep[:, D:], 1)
    grad = is_grad_row((ROWS, 128))
    own = jnp.where(
        grad,
        pack_stats([jnp.zeros_like(peak), jnp.zeros_like(peak), column_dot]),
        pack_stats([peak, total, jnp.zeros_like(peak)]),
    )
    stats = (own + swap_halves(own, grad)).astype(bf16)
    for d in range(16):
        out[d, :, :D] = low
        out[d, :, D:] = stats


def logit_body(tokens, cot, lt_ref, gm, gt, r_mine, r_theirs, dl_ref, w_ref, g_ref):
    grad = is_grad_row((256, TOK))
    g_mine = gm[...].astype(f32)
    g_theirs = gt[...].astype(f32)
    for c in range(CLIPS):
        rows = slice(8 * c, 8 * c + 8)
        both = jnp.concatenate(
            [g_mine[:, rows].reshape(128, WIDE), g_theirs[:, rows].reshape(128, WIDE)], axis=0
        )
        stats = both[:, D:]
        low = both[:, :D].astype(bf16)
        g_ref[c] = low
        peak, total, column_dot = (read_stat(stats, i) for i in range(3))
        logits = lt_ref[c]
        raised = jnp.exp(logits - jnp.max(logits, axis=0, keepdims=True))
        combine = raised / (0.5 * jnp.sum(raised, axis=0, keepdims=True))
        combine = jnp.where(grad, 0.0, combine)
        d_combine = dot(low, cot[c], NT)
        inner = jnp.sum(combine * d_combine, axis=0, keepdims=True)
        dispatch = jnp.where(grad, jnp.exp(logits - peak) * (1.0 / total), 0.0)
        d_dispatch = dot(low, tokens[c], NT)
        own = jnp.where(grad, dispatch * (d_dispatch - column_dot), combine * (d_combine - inner))
        d_logit = (own + swap_halves(own, grad)).astype(bf16)
        part = dot(d_logit, tokens[c])
        grad_half = is_grad_row((256, 640))
        part = jnp.where(grad_half, part[:, 640:], part[:, :640]).reshape(32, 8, 640)
        if c == 0:
            r_mine[...] = part[:16]
            r_theirs[...] = part[16:]
        else:
            r_mine[...] += part[:16]
            r_theirs[...] += part[16:]
        dl_ref[c] = jnp.where(grad, 0.0, d_logit.astype(f32)).astype(bf16)
        w_ref[c] = dispatch.astype(bf16)


def tokens_body(dl_ref, w_ref, rt_ref, g_ref, out):
    for c in range(CLIPS):
        out[c] = (dot(dl_ref[c], rt_ref[...], TN) + dot(w_ref[c], g_ref[c], TN)).astype(bf16)


def add_body(a_ref, b_ref, out):
    out[...] = a_ref[...] + b_ref[...]


def spread_body(x_ref, out):
    acc = x_ref[0]
    for i in range(1, x_ref.shape[0]):
        acc = acc + x_ref[i]
    for i in range(out.shape[0]):
        out[i] = acc


def router_body(core_ref, mine, theirs, out):
    t = lax.broadcasted_iota(jnp.int32, (256, 128), 0)
    s = lax.broadcasted_iota(jnp.int32, (256, 128), 1)
    half = t // 128
    owner_core = half + core_ref[0] * (1 - 2 * half)
    slot = 8 * ((t % 128) // 8) + 4 * owner_core + t % 4
    rows = jnp.concatenate([mine[...].reshape(128, 640), theirs[...].reshape(128, 640)], axis=0)
    high = rows.astype(bf16)
    rest = rows - high.astype(f32)
    middle = rest.astype(bf16)
    low = (rest - middle.astype(f32)).astype(bf16)
    for a in range(2):
        pick = ((s == slot) & ((t % 8) // 4 == a)).astype(f32).astype(bf16)
        moved = dot(high, pick, TN) + (dot(middle, pick, TN) + dot(low, pick, TN))
        out[a * 640 : (a + 1) * 640, :] = moved


def exchange(x, axes):
    return lax.all_to_all(x, axes, 0, 0, tiled=True)


def to_partner(x):
    return lax.ppermute(x, "core", [(0, 1), (1, 0)])


def per_device(tokens, router, w_in, w_out, cotangent):
    core = lax.axis_index("core").astype(jnp.int32).reshape(1)
    block = ((16, ROWS, WIDE), bf16)
    mine, theirs, rt, lt = call(
        slots_body,
        [block, block, ((256, D), bf16), ((CLIPS, 256, TOK), f32)],
        core,
        tokens,
        router,
        cotangent,
        scratch=[pltpu.VMEM((CLIPS, 256, TOK), bf16), pltpu.VMEM((CLIPS, 256, TOK), bf16)],
        smem=(0,),
        flops=3 * 10**9,
        nbytes=8 * 10**6,
    )
    (summed,) = call(pair_body, [block], mine, to_partner(theirs), nbytes=3 * 10**6)
    owned = exchange(summed, OWNERS)
    (owned,) = call(owner_body, [((8, ROWS, WIDE), bf16)], owned, nbytes=2 * 10**6)
    shared = exchange(owned, EXP)
    parts, keep = call(
        expert_body,
        [((8, ROWS, D), bf16), ((ROWS, WIDE), f32)],
        shared,
        w_in,
        w_out,
        flops=10**9,
        nbytes=8 * 10**6,
    )
    parts = exchange(parts, EXP)
    (result,) = call(result_body, [block], parts, keep, nbytes=2 * 10**6)
    g_mine = exchange(result, OWNERS)
    g_theirs = to_partner(g_mine)
    half = ((16, 8, 640), f32)
    square = ((CLIPS, 256, TOK), bf16)
    r_mine, r_theirs, d_logit, dispatch, grads = call(
        logit_body,
        [half, half, square, square, ((CLIPS, 256, D), bf16)],
        tokens,
        cotangent,
        lt,
        g_mine,
        g_theirs,
        flops=3 * 10**9,
        nbytes=10**7,
    )
    (r_mine,) = call(add_body, [half], r_mine, to_partner(r_theirs), nbytes=10**6)
    (d_tokens,) = call(
        tokens_body,
        [((CLIPS, TOK, D), bf16)],
        d_logit,
        dispatch,
        rt,
        grads,
        flops=10**9,
        nbytes=6 * 10**6,
    )
    r_mine = exchange(r_mine, PLANE)
    (r_mine,) = call(spread_body, [((8, 8, 640), f32)], r_mine, nbytes=10**6)
    r_mine = exchange(r_mine, ("z",))
    (r_mine,) = call(spread_body, [half], r_mine, nbytes=10**6)
    r_mine = exchange(r_mine, PLANE)
    (d_router,) = call(
        router_body, [((D, 128), f32)], core, r_mine, to_partner(r_mine), smem=(0,), nbytes=2 * 10**6
    )
    return (d_tokens, d_router)


def solution(mesh):
    fine = Mesh(mesh.devices.reshape(tuple(SIZES.values())), AXES)
    seq = ("yl", "z", "core")
    placed = (
        P(None, AXES, None),
        P(),
        P(seq, None, EXP),
        P(seq, EXP, None),
        P(None, AXES, None),
    )
    return jax.shard_map(
        per_device,
        mesh=fine,
        in_specs=placed,
        out_specs=(P(None, AXES, None), P()),
        check_vma=False,
    )
```

```python
import functools

import jax
import jax.numpy as jnp
from jax import lax
from jax.experimental import pallas as pl
from jax.experimental.pallas import tpu as pltpu
from jax.sharding import Mesh, PartitionSpec as P

SIZES = {"yl": 2, "z": 8, "core": 2, "yh": 2, "x": 4}
AXES = tuple(SIZES)
OWNERS = ("yl", "z")
EXP = ("yh", "x")
PLANE = ("yl", "yh", "x")

D = 1280
CLIPS = 3
TOK = 256
ROWS = 24
PART = 512
STAT = 96
MiB = 1024 * 1024
GELU_C = 0.7978845608028654
GELU_A = 0.044715

bf16 = jnp.bfloat16
f32 = jnp.float32

NT = (((1,), (1,)), ((), ()))
TN = (((0,), (0,)), ((), ()))


def dot(a, b, dims=None):
    if dims is None:
        return jnp.dot(a, b, preferred_element_type=f32)
    return lax.dot_general(a, b, dims, preferred_element_type=f32)


def is_grad_row(shape):
    return lax.broadcasted_iota(jnp.int32, shape, 0) % 8 >= 4


def swap_halves(v, grad):
    n = v.shape[0]
    return jnp.where(grad, pltpu.roll(v, 4, 0), pltpu.roll(v, n - 4, 0))


def lanes_of(shape):
    return lax.broadcasted_iota(jnp.int32, shape, len(shape) - 1)


def split(value):
    high = value.astype(bf16).astype(f32)
    rest = value - high
    middle = rest.astype(bf16).astype(f32)
    return high, middle, rest - middle


def spread_triple(value):
    high, middle, low = split(value)
    return high + pltpu.roll(middle, 1, 1) + pltpu.roll(low, 2, 1)


def join_triple(stats):
    return stats + pltpu.roll(stats, 127, 1) + pltpu.roll(stats, 126, 1)


def clip_columns(x):
    return [x[:, STAT + 8 * c : STAT + 8 * c + 1] for c in range(CLIPS)]


def by_quarter(columns, lane):
    first = jnp.where(lane < 32, columns[0], columns[1])
    return jnp.where(lane < 64, first, columns[2])


def merge_stats(last):
    joined = [join_triple(x) for x in last]
    peak = functools.reduce(jnp.maximum, joined)
    scales = [jnp.exp(jnp.minimum(j - peak, 0.0)) for j in joined]
    total = functools.reduce(jnp.add, [pltpu.roll(x, 3, 1) * j for x, j in zip(scales, joined)])
    lane = lanes_of(peak.shape)
    stats = jnp.where(lane % 8 == 0, peak, jnp.where(lane % 8 == 3, total, 0.0))
    stats = spread_triple(jnp.where(lane < STAT, 0.0, stats))
    return [clip_columns(x) for x in scales], stats


def merge_tiles(wide, columns, stats):
    tiles = []
    for c in range(CLIPS):
        lanes = slice(128 * c, 128 * c + 128)
        parts = [col[c] * b[:, lanes] for b, col in zip(wide, columns)]
        tiles.append(functools.reduce(jnp.add, parts))
    lane = lanes_of(stats.shape)
    parts = [by_quarter(col, lane) * b[:, 384:] for b, col in zip(wide, columns)]
    tiles.append(jnp.where(lane < STAT, functools.reduce(jnp.add, parts), stats))
    return jnp.concatenate(tiles, axis=1)


def merge_blocks(blocks):
    wide = [b.astype(f32) for b in blocks]
    return merge_tiles(wide, *merge_stats([b[:, 384:] for b in wide]))


def rows_of(blocks, c):
    lane = lanes_of((blocks[0].shape[0], 128))
    tiles = [b[:, 128 * c : 128 * c + 128] for b in blocks]
    for first in (0, 4):
        tile = None
        for q in range(4):
            turned = blocks[first + q][:, 384:]
            if q != c:
                turned = pltpu.roll(turned, 32 * (q - c) % 128, 1)
            tile = turned if tile is None else jnp.where(lane // 32 == q, turned, tile)
        tiles.append(tile)
    return jnp.concatenate(tiles, axis=1)


def last_tile(tails, j, stats):
    lane = lanes_of(stats.shape)
    out = stats
    for c, tail in enumerate(tails):
        tile = tail[:, 128 * (j // 4) : 128 * (j // 4) + 128]
        if j % 4 != c:
            tile = pltpu.roll(tile, 32 * (c - j % 4) % 128, 1)
        out = jnp.where(lane // 32 == c, tile, out)
    return out


def call(body, outs, *args, scratch=(), flops=0, nbytes=0, smem=(), hbm=(), limit=16):
    spaces = [
        pltpu.SMEM if i in smem else pltpu.HBM if i in hbm else pltpu.VMEM for i in range(len(args))
    ]
    return pl.pallas_call(
        body,
        out_shape=[jax.ShapeDtypeStruct(s, t) for s, t in outs],
        in_specs=[pl.BlockSpec(memory_space=s) for s in spaces],
        out_specs=[pl.BlockSpec(memory_space=pltpu.VMEM) for _ in outs],
        scratch_shapes=list(scratch),
        compiler_params=pltpu.CompilerParams(vmem_limit_bytes=limit * MiB),
        cost_estimate=pl.CostEstimate(flops=flops, bytes_accessed=nbytes, transcendentals=0),
    )(*args)


def slot_of_row(core):
    t = lax.broadcasted_iota(jnp.int32, (256, 128), 0)
    s = lax.broadcasted_iota(jnp.int32, (256, 128), 1)
    half = t // 128
    slot = 8 * ((t % 128) // 8) + 4 * (half + core * (1 - 2 * half)) + t % 4
    return s == slot, t


def slots_body(
    core_ref, router_hbm, tokens_hbm, cot_hbm, mine, theirs, rt_ref, lt_ref,
    router, tokens, cot, weights_in, weights_out, sems, router_sem,
):
    first = pltpu.make_async_copy(router_hbm, router, router_sem)
    copies = [
        pltpu.make_async_copy(src.at[c], dst.at[c], sems.at[i, c])
        for i, (src, dst) in enumerate(((tokens_hbm, tokens), (cot_hbm, cot)))
        for c in range(CLIPS)
    ]
    first.start()
    for copy in copies:
        copy.start()
    pick, _ = slot_of_row(core_ref[0])
    pick = pick.astype(f32).astype(bf16)
    first.wait()
    rt_ref[...] = dot(pick, router[...], NT).astype(bf16)
    grad = is_grad_row((256, TOK))
    lane = lanes_of((256, 128))
    stats = jnp.zeros((256, 128), f32)
    for c in range(CLIPS):
        copies[c].wait()
        logits = dot(rt_ref[...], tokens[c], NT)
        lt_ref[c] = logits
        peak = jnp.max(logits, axis=1, keepdims=True)
        low = jnp.where(grad, 0.0, jnp.exp(logits - peak)).astype(bf16)
        total = jnp.sum(low.astype(f32), axis=1, keepdims=True)
        weights_in[c] = low
        raised = jnp.exp(logits - jnp.max(logits, axis=0, keepdims=True))
        combine = raised * (2.0 / jnp.sum(raised, axis=0, keepdims=True))
        weights_out[c] = jnp.where(grad, combine, 0.0).astype(bf16)
        at = STAT + 8 * c
        stats = jnp.where(lane == at, peak, jnp.where(lane == at + 3, total, stats))
    ones = jnp.where((lane >= STAT) & (lane % 8 == 3), 1.0, 0.0)
    stats = spread_triple(jnp.where(is_grad_row((256, 128)), ones, stats))

    def product(c, lanes):
        return dot(weights_in[c], tokens[c, :, lanes]) + dot(weights_out[c], cot[c, :, lanes])

    for c in range(CLIPS):
        copies[CLIPS + c].wait()
        for i in range(4):
            part = product(c, slice(256 * i, 256 * i + 256)).reshape(32, 8, 256)
            for h in range(2):
                tile = part[:, :, 128 * h : 128 * h + 128]
                mine[2 * i + h, :, :, 128 * c : 128 * c + 128] = tile[:16]
                theirs[2 * i + h, :, :, 128 * c : 128 * c + 128] = tile[16:].astype(bf16)
    tails = [product(c, slice(1024, 1280)) for c in range(CLIPS)]
    for j in range(8):
        tile = last_tile(tails, j, stats).reshape(32, 8, 128)
        mine[j, :, :, 384:] = tile[:16]
        theirs[j, :, :, 384:] = tile[16:].astype(bf16)


def pair_body(a_ref, b_ref, out):
    columns, stats = merge_stats([x[0, :, :, 384:].astype(f32).reshape(128, 128) for x in (a_ref, b_ref)])
    for j in range(8):
        wide = [x[j].astype(f32).reshape(128, PART) for x in (a_ref, b_ref)]
        out[j] = merge_tiles(wide, columns, stats).astype(bf16).reshape(16, 8, PART)


def members_body(x_ref, out):
    blocks = [x_ref[e].astype(f32).reshape(128, PART) for e in range(8)]
    out[...] = merge_blocks(blocks).reshape(16, 8, PART)


def owner_body(x_ref, out, own):
    merged = merge_blocks([x_ref[d] for d in range(16)])
    last = merged[:, 384:]
    joined = join_triple(last)
    grad = is_grad_row((8, 1))
    totals = [joined[:, STAT + 8 * c + 3 : STAT + 8 * c + 4] for c in range(CLIPS)]
    inverse = [jnp.where(grad, 1.0, 1.0 / total) for total in totals]
    lane = lanes_of(last.shape)
    tiles = [merged[:, 128 * c : 128 * c + 128] * inverse[c] for c in range(CLIPS)]
    tiles.append(jnp.where(lane < STAT, last * by_quarter(inverse, lane), last))
    rows = jnp.concatenate(tiles, axis=1)
    own[...] = rows
    low = rows.astype(bf16)
    for e in range(8):
        out[e] = low


def gelu_parts(v):
    t = jnp.tanh(GELU_C * (v + GELU_A * (v * v * v)))
    value = 0.5 * v * (1.0 + t)
    slope = 0.5 * (1.0 + t) + 0.5 * v * (1.0 - t * t) * (GELU_C * (1.0 + 3.0 * GELU_A * (v * v)))
    return value, slope


def expert_body(x_ref, w_in, w_out, out, stats_out):
    blocks = [x_ref[e].astype(f32) for e in range(8)]
    stats_out[...] = join_triple(blocks[0][:, 384:])
    low = jnp.concatenate([rows_of(blocks, c) for c in range(CLIPS)], axis=0).astype(bf16)
    row = lax.broadcasted_iota(jnp.int32, (ROWS, 640), 0)
    grad = row % 8 >= 4
    acc = jnp.zeros((ROWS, D), f32)
    for i in range(2):
        own = (row % 4) // 2 == i
        value, slope = gelu_parts(dot(low, w_in[i]))
        d_pre = dot(low, w_out[i], NT) * pltpu.roll(slope, 4, 0)
        hidden = jnp.where(own & jnp.logical_not(grad), value, 0.0).astype(bf16)
        d_pre = jnp.where(own & grad, d_pre, 0.0).astype(bf16)
        acc = acc + dot(hidden, w_out[i]) + dot(d_pre, w_in[i], NT)
    by_clip = [acc[8 * c : 8 * c + 8] for c in range(CLIPS)]
    tails = [rows[:, 1024:] for rows in by_clip]
    empty = jnp.zeros((8, 128), f32)
    for j in range(8):
        tiles = [rows[:, 128 * j : 128 * j + 128] for rows in by_clip]
        out[j] = jnp.concatenate(tiles + [last_tile(tails, j, empty)], axis=1)


def result_body(x_ref, joined, own, out):
    acc = x_ref[0]
    for e in range(1, 8):
        acc = acc + x_ref[e]
    low = acc.astype(bf16).astype(f32)
    products = low * pltpu.roll(own[...], 4, 0)
    lane = lanes_of((8, 128))
    grad = is_grad_row((8, 128))
    kept = jnp.where((lane % 8 == 0) | (lane % 8 == 3), joined[...], 0.0)
    dots = jnp.zeros((8, 128), f32)
    for c in range(CLIPS):
        both = products[:, 128 * c : 128 * c + 128]
        both = both + jnp.where(lane // 32 == c, products[:, 384:], 0.0)
        total = jnp.sum(both, axis=1, keepdims=True)
        dots = jnp.where(lane == STAT + 8 * c, total, dots)
    stats = spread_triple(jnp.where(lane < STAT, 0.0, jnp.where(grad, dots, kept)))
    last = jnp.where(lane < STAT, low[:, 384:], stats)
    full = jnp.concatenate([low[:, :384], last], axis=1).astype(bf16)
    for d in range(16):
        out[d] = full


def copies_body(x_ref, out):
    for e in range(8):
        out[e] = x_ref[...]


def logit_body(tokens, cot, lt_ref, gm, gt, r_mine, r_theirs, dl_ref, w_ref, g_ref, r_sum):
    grad = is_grad_row((256, TOK))
    grad_half = is_grad_row((256, 640))
    halves = [[g[j].astype(f32).reshape(128, PART) for j in range(8)] for g in (gm, gt)]
    dots = [functools.reduce(jnp.add, [part[:, 384:] for part in h]) for h in halves]
    dots = join_triple(jnp.concatenate(dots, axis=0))
    stats = join_triple(jnp.concatenate([h[0][:, 384:] for h in halves], axis=0))
    stats = pltpu.roll(stats, 4, 0)
    for c in range(CLIPS):
        low = jnp.concatenate([rows_of(h, c).astype(bf16) for h in halves], axis=0)
        g_ref[c] = low
        at = STAT + 8 * c
        peak = stats[:, at : at + 1]
        total = stats[:, at + 3 : at + 4]
        column_dot = dots[:, at : at + 1]
        logits = lt_ref[c]
        raised = jnp.exp(logits - jnp.max(logits, axis=0, keepdims=True))
        combine = raised * (2.0 / jnp.sum(raised, axis=0, keepdims=True))
        combine = jnp.where(grad, 0.0, combine)
        d_combine = dot(low, cot[c], NT)
        inner = jnp.sum(combine * d_combine, axis=0, keepdims=True)
        dispatch = jnp.where(grad, jnp.exp(logits - peak) * (1.0 / total), 0.0)
        d_dispatch = dot(low, tokens[c], NT)
        own = jnp.where(grad, dispatch * (d_dispatch - column_dot), combine * (d_combine - inner))
        d_logit = (own + swap_halves(own, grad)).astype(bf16)
        part = dot(d_logit, tokens[c])
        part = jnp.where(grad_half, part[:, 640:], part[:, :640])
        if c == 0:
            r_sum[...] = part
        else:
            r_sum[...] += part
        dl_ref[c] = jnp.where(grad, 0.0, d_logit.astype(f32)).astype(bf16)
        w_ref[c] = dispatch.astype(bf16)
    r_mine[...] = r_sum[:128].astype(bf16).reshape(16, 8, 640)
    r_theirs[...] = r_sum[128:].astype(bf16).reshape(16, 8, 640)


def tokens_body(dl_ref, w_ref, rt_ref, g_ref, out):
    for c in range(CLIPS):
        out[c] = (dot(dl_ref[c], rt_ref[...], TN) + dot(w_ref[c], g_ref[c], TN)).astype(bf16)


def add_body(a_ref, b_ref, out):
    out[...] = (a_ref[...].astype(f32) + b_ref[...].astype(f32)).astype(bf16)


def spread_body(x_ref, out):
    acc = x_ref[0].astype(f32)
    for i in range(1, x_ref.shape[0]):
        acc = acc + x_ref[i].astype(f32)
    acc = acc.astype(bf16)
    for i in range(out.shape[0]):
        out[i] = acc


def router_body(core_ref, mine, theirs, out):
    hit, t = slot_of_row(core_ref[0])
    rows = [x[...].astype(f32).reshape(128, 640) for x in (mine, theirs)]
    rows = jnp.concatenate(rows, axis=0).astype(bf16)
    for a in range(2):
        pick = (hit & ((t % 8) // 4 == a)).astype(f32).astype(bf16)
        out[a * 640 : (a + 1) * 640, :] = dot(rows, pick, TN)


def exchange(x, axes):
    return lax.all_to_all(x, axes, 0, 0, tiled=True)


def to_partner(x):
    return lax.ppermute(x, "core", [(0, 1), (1, 0)])


def per_device(tokens, router, w_in, w_out, cotangent):
    core = lax.axis_index("core").astype(jnp.int32).reshape(1)
    values = ((8, 16, 8, PART), bf16)
    local = (CLIPS, TOK, D)
    square = ((CLIPS, 256, TOK), bf16)
    mine, theirs, rt, lt = call(
        slots_body,
        [(values[0], f32), values, ((256, D), bf16), ((CLIPS, 256, TOK), f32)],
        core,
        *[pltpu.with_memory_space_constraint(x, pltpu.HBM) for x in (router, tokens, cotangent)],
        scratch=[
            pltpu.VMEM((D, 128), bf16),
            pltpu.VMEM(local, bf16),
            pltpu.VMEM(local, bf16),
            pltpu.VMEM(*square),
            pltpu.VMEM(*square),
            pltpu.SemaphoreType.DMA((2, CLIPS)),
            pltpu.SemaphoreType.DMA,
        ],
        smem=(0,),
        hbm=(1, 2, 3),
        flops=3 * 10**9,
        nbytes=8 * 10**6,
        limit=24,
    )
    (sums,) = call(pair_body, [values], mine, to_partner(theirs), flops=10**10, nbytes=3 * 10**6)
    (sums,) = call(
        members_body, [((16, 8, PART), f32)], exchange(sums, EXP), flops=10**10, nbytes=10**6
    )
    sums, own = call(
        owner_body,
        [((8, 8, PART), bf16), ((8, PART), f32)],
        exchange(sums, OWNERS),
        nbytes=10**5,
    )
    parts, stats = call(
        expert_body,
        [((8, 8, PART), f32), ((8, 128), f32)],
        exchange(sums, EXP),
        w_in,
        w_out,
        flops=10**9,
        nbytes=8 * 10**6,
    )
    (result,) = call(
        result_body, [((16, 8, PART), bf16)], exchange(parts, EXP), stats, own, nbytes=10**5
    )
    (result,) = call(copies_body, [values], exchange(result, OWNERS), nbytes=10**6)
    g_mine = exchange(result, EXP)
    g_theirs = to_partner(g_mine)
    half = ((16, 8, 640), bf16)
    r_mine, r_theirs, d_logit, dispatch, grads = call(
        logit_body,
        [half, half, square, square, (local, bf16)],
        tokens,
        cotangent,
        lt,
        g_mine,
        g_theirs,
        scratch=[pltpu.VMEM((256, 640), f32)],
        flops=3 * 10**9,
        nbytes=10**7,
        limit=24,
    )
    (r_mine,) = call(add_body, [half], r_mine, to_partner(r_theirs), nbytes=10**6)
    (d_tokens,) = call(
        tokens_body, [(local, bf16)], d_logit, dispatch, rt, grads, flops=10**9, nbytes=6 * 10**6
    )
    r_mine = exchange(r_mine, PLANE)
    (r_mine,) = call(spread_body, [((8, 8, 640), bf16)], r_mine, nbytes=10**5)
    r_mine = exchange(r_mine, ("z",))
    (r_mine,) = call(spread_body, [half], r_mine, nbytes=10**5)
    r_mine = exchange(r_mine, PLANE)
    (d_router,) = call(
        router_body, [((D, 128), f32)], core, r_mine, to_partner(r_mine), smem=(0,), nbytes=2 * 10**6
    )
    return (d_tokens, d_router)


def solution(mesh):
    fine = Mesh(mesh.devices.reshape(tuple(SIZES.values())), AXES)
    seq = ("yl", "z", "core")
    placed = (
        P(None, AXES, None),
        P(),
        P(seq, None, EXP),
        P(seq, EXP, None),
        P(None, AXES, None),
    )
    return jax.shard_map(
        per_device,
        mesh=fine,
        in_specs=placed,
        out_specs=(P(None, AXES, None), P()),
        check_vma=False,
    )
```

```python
import functools

import jax
import jax.numpy as jnp
from jax import lax
from jax.experimental import pallas as pl
from jax.experimental.pallas import tpu as pltpu
from jax.sharding import Mesh, PartitionSpec as P

SIZES = {"yl": 2, "z": 8, "core": 2, "yh": 2, "x": 4}
AXES = tuple(SIZES)
EXP = ("yh", "x")
PLANE = ("yl", "yh", "x")

D = 1280
CLIPS = 3
TOK = 256
ROWS = 24
PART = 512
STAT = 96
MiB = 1024 * 1024
GELU_C = 0.7978845608028654
GELU_A = 0.044715

bf16 = jnp.bfloat16
f32 = jnp.float32

NT = (((1,), (1,)), ((), ()))
TN = (((0,), (0,)), ((), ()))


def dot(a, b, dims=None):
    if dims is None:
        return jnp.dot(a, b, preferred_element_type=f32)
    return lax.dot_general(a, b, dims, preferred_element_type=f32)


def is_grad_row(shape):
    return lax.broadcasted_iota(jnp.int32, shape, 0) % 8 >= 4


def swap_halves(v, grad):
    n = v.shape[0]
    return jnp.where(grad, pltpu.roll(v, 4, 0), pltpu.roll(v, n - 4, 0))


def lanes_of(shape):
    return lax.broadcasted_iota(jnp.int32, shape, len(shape) - 1)


def split(value):
    high = value.astype(bf16).astype(f32)
    rest = value - high
    middle = rest.astype(bf16).astype(f32)
    return high, middle, rest - middle


def spread_triple(value):
    high, middle, low = split(value)
    return high + pltpu.roll(middle, 1, 1) + pltpu.roll(low, 2, 1)


def join_triple(stats):
    return stats + pltpu.roll(stats, 127, 1) + pltpu.roll(stats, 126, 1)


def clip_columns(x):
    return [x[:, STAT + 8 * c : STAT + 8 * c + 1] for c in range(CLIPS)]


def by_quarter(columns, lane):
    first = jnp.where(lane < 32, columns[0], columns[1])
    return jnp.where(lane < 64, first, columns[2])


def merge_stats(last):
    joined = [join_triple(x) for x in last]
    peak = functools.reduce(jnp.maximum, joined)
    scales = [jnp.exp(jnp.minimum(j - peak, 0.0)) for j in joined]
    total = functools.reduce(jnp.add, [pltpu.roll(x, 3, 1) * j for x, j in zip(scales, joined)])
    lane = lanes_of(peak.shape)
    stats = jnp.where(lane % 8 == 0, peak, jnp.where(lane % 8 == 3, total, 0.0))
    stats = spread_triple(jnp.where(lane < STAT, 0.0, stats))
    return [clip_columns(x) for x in scales], stats


def merge_tiles(wide, columns, stats):
    tiles = []
    for c in range(CLIPS):
        lanes = slice(128 * c, 128 * c + 128)
        parts = [col[c] * b[:, lanes] for b, col in zip(wide, columns)]
        tiles.append(functools.reduce(jnp.add, parts))
    lane = lanes_of(stats.shape)
    parts = [by_quarter(col, lane) * b[:, 384:] for b, col in zip(wide, columns)]
    tiles.append(jnp.where(lane < STAT, functools.reduce(jnp.add, parts), stats))
    return jnp.concatenate(tiles, axis=1)


def merge_blocks(blocks):
    wide = [b.astype(f32) for b in blocks]
    return merge_tiles(wide, *merge_stats([b[:, 384:] for b in wide]))


def rows_of(blocks, c):
    lane = lanes_of((blocks[0].shape[0], 128))
    tiles = [b[:, 128 * c : 128 * c + 128] for b in blocks]
    for first in (0, 4):
        tile = None
        for q in range(4):
            turned = blocks[first + q][:, 384:]
            if q != c:
                turned = pltpu.roll(turned, 32 * (q - c) % 128, 1)
            tile = turned if tile is None else jnp.where(lane // 32 == q, turned, tile)
        tiles.append(tile)
    return jnp.concatenate(tiles, axis=1)


def last_tile(tails, j, stats):
    lane = lanes_of(stats.shape)
    out = stats
    for c, tail in enumerate(tails):
        tile = tail[:, 128 * (j // 4) : 128 * (j // 4) + 128]
        if j % 4 != c:
            tile = pltpu.roll(tile, 32 * (c - j % 4) % 128, 1)
        out = jnp.where(lane // 32 == c, tile, out)
    return out


def call(body, outs, *args, scratch=(), flops=0, nbytes=0, smem=(), hbm=(), limit=16):
    spaces = [
        pltpu.SMEM if i in smem else pltpu.HBM if i in hbm else pltpu.VMEM for i in range(len(args))
    ]
    return pl.pallas_call(
        body,
        out_shape=[jax.ShapeDtypeStruct(s, t) for s, t in outs],
        in_specs=[pl.BlockSpec(memory_space=s) for s in spaces],
        out_specs=[pl.BlockSpec(memory_space=pltpu.VMEM) for _ in outs],
        scratch_shapes=list(scratch),
        compiler_params=pltpu.CompilerParams(vmem_limit_bytes=limit * MiB),
        cost_estimate=pl.CostEstimate(flops=flops, bytes_accessed=nbytes, transcendentals=0),
    )(*args)


def slot_of_row(core):
    t = lax.broadcasted_iota(jnp.int32, (256, 128), 0)
    s = lax.broadcasted_iota(jnp.int32, (256, 128), 1)
    half = t // 128
    slot = 8 * ((t % 128) // 8) + 4 * (half + core * (1 - 2 * half)) + t % 4
    return s == slot, t


def slots_body(
    core_ref, router_hbm, tokens_hbm, cot_hbm, mine, theirs, rt_ref, lt_ref,
    router, tokens, cot, weights_in, weights_out, sems, router_sem,
):
    first = pltpu.make_async_copy(router_hbm, router, router_sem)
    copies = [
        pltpu.make_async_copy(src.at[c], dst.at[c], sems.at[i, c])
        for i, (src, dst) in enumerate(((tokens_hbm, tokens), (cot_hbm, cot)))
        for c in range(CLIPS)
    ]
    first.start()
    for copy in copies:
        copy.start()
    pick, _ = slot_of_row(core_ref[0])
    pick = pick.astype(f32).astype(bf16)
    first.wait()
    rt_ref[...] = dot(pick, router[...], NT).astype(bf16)
    grad = is_grad_row((256, TOK))
    lane = lanes_of((256, 128))
    stats = jnp.zeros((256, 128), f32)
    for c in range(CLIPS):
        copies[c].wait()
        logits = dot(rt_ref[...], tokens[c], NT)
        lt_ref[c] = logits
        peak = jnp.max(logits, axis=1, keepdims=True)
        low = jnp.where(grad, 0.0, jnp.exp(logits - peak)).astype(bf16)
        total = jnp.sum(low.astype(f32), axis=1, keepdims=True)
        weights_in[c] = low
        raised = jnp.exp(logits - jnp.max(logits, axis=0, keepdims=True))
        combine = raised * (2.0 / jnp.sum(raised, axis=0, keepdims=True))
        weights_out[c] = jnp.where(grad, combine, 0.0).astype(bf16)
        at = STAT + 8 * c
        stats = jnp.where(lane == at, peak, jnp.where(lane == at + 3, total, stats))
    ones = jnp.where((lane >= STAT) & (lane % 8 == 3), 1.0, 0.0)
    stats = spread_triple(jnp.where(is_grad_row((256, 128)), ones, stats))

    def product(c, lanes):
        return dot(weights_in[c], tokens[c, :, lanes]) + dot(weights_out[c], cot[c, :, lanes])

    for c in range(CLIPS):
        copies[CLIPS + c].wait()
        for i in range(4):
            part = product(c, slice(256 * i, 256 * i + 256)).reshape(32, 8, 256)
            for h in range(2):
                tile = part[:, :, 128 * h : 128 * h + 128]
                mine[2 * i + h, :, :, 128 * c : 128 * c + 128] = tile[:16]
                theirs[2 * i + h, :, :, 128 * c : 128 * c + 128] = tile[16:].astype(bf16)
    tails = [product(c, slice(1024, 1280)) for c in range(CLIPS)]
    for j in range(8):
        tile = last_tile(tails, j, stats).reshape(32, 8, 128)
        mine[j, :, :, 384:] = tile[:16]
        theirs[j, :, :, 384:] = tile[16:].astype(bf16)


def pair_body(a_ref, b_ref, out):
    columns, stats = merge_stats([x[0, :, :, 384:].astype(f32).reshape(128, 128) for x in (a_ref, b_ref)])
    for j in range(8):
        wide = [x[j].astype(f32).reshape(128, PART) for x in (a_ref, b_ref)]
        merged = merge_tiles(wide, columns, stats).astype(bf16)
        out[j] = merged[:64].reshape(8, 8, PART)
        out[8 + j] = merged[64:].reshape(8, 8, PART)


def members_body(x_ref, out):
    blocks = [x_ref[e].astype(f32).reshape(64, PART) for e in range(16)]
    out[...] = merge_blocks(blocks).reshape(8, 8, PART)


def owner_body(x_ref, out, own):
    merged = merge_blocks([x_ref[z] for z in range(8)])
    last = merged[:, 384:]
    joined = join_triple(last)
    grad = is_grad_row((8, 1))
    totals = [joined[:, STAT + 8 * c + 3 : STAT + 8 * c + 4] for c in range(CLIPS)]
    inverse = [jnp.where(grad, 1.0, 1.0 / total) for total in totals]
    lane = lanes_of(last.shape)
    tiles = [merged[:, 128 * c : 128 * c + 128] * inverse[c] for c in range(CLIPS)]
    tiles.append(jnp.where(lane < STAT, last * by_quarter(inverse, lane), last))
    rows = jnp.concatenate(tiles, axis=1)
    own[...] = rows
    low = rows.astype(bf16)
    for e in range(8):
        out[e] = low


def gelu_parts(v):
    t = jnp.tanh(GELU_C * (v + GELU_A * (v * v * v)))
    value = 0.5 * v * (1.0 + t)
    slope = 0.5 * (1.0 + t) + 0.5 * v * (1.0 - t * t) * (GELU_C * (1.0 + 3.0 * GELU_A * (v * v)))
    return value, slope


def expert_body(x_ref, w_in, w_out, out, stats_out):
    blocks = [x_ref[e].astype(f32) for e in range(8)]
    stats_out[...] = join_triple(blocks[0][:, 384:])
    low = jnp.concatenate([rows_of(blocks, c) for c in range(CLIPS)], axis=0).astype(bf16)
    row = lax.broadcasted_iota(jnp.int32, (ROWS, 640), 0)
    grad = row % 8 >= 4
    acc = jnp.zeros((ROWS, D), f32)
    for i in range(2):
        own = (row % 4) // 2 == i
        value, slope = gelu_parts(dot(low, w_in[i]))
        d_pre = dot(low, w_out[i], NT) * pltpu.roll(slope, 4, 0)
        hidden = jnp.where(own & jnp.logical_not(grad), value, 0.0).astype(bf16)
        d_pre = jnp.where(own & grad, d_pre, 0.0).astype(bf16)
        acc = acc + dot(hidden, w_out[i]) + dot(d_pre, w_in[i], NT)
    by_clip = [acc[8 * c : 8 * c + 8] for c in range(CLIPS)]
    tails = [rows[:, 1024:] for rows in by_clip]
    empty = jnp.zeros((8, 128), f32)
    for j in range(8):
        tiles = [rows[:, 128 * j : 128 * j + 128] for rows in by_clip]
        out[j] = jnp.concatenate(tiles + [last_tile(tails, j, empty)], axis=1)


def result_body(x_ref, joined, own, out):
    acc = x_ref[0]
    for e in range(1, 8):
        acc = acc + x_ref[e]
    low = acc.astype(bf16).astype(f32)
    products = low * pltpu.roll(own[...], 4, 0)
    lane = lanes_of((8, 128))
    grad = is_grad_row((8, 128))
    kept = jnp.where((lane % 8 == 0) | (lane % 8 == 3), joined[...], 0.0)
    dots = jnp.zeros((8, 128), f32)
    for c in range(CLIPS):
        both = products[:, 128 * c : 128 * c + 128]
        both = both + jnp.where(lane // 32 == c, products[:, 384:], 0.0)
        total = jnp.sum(both, axis=1, keepdims=True)
        dots = jnp.where(lane == STAT + 8 * c, total, dots)
    stats = spread_triple(jnp.where(lane < STAT, 0.0, jnp.where(grad, dots, kept)))
    last = jnp.where(lane < STAT, low[:, 384:], stats)
    full = jnp.concatenate([low[:, :384], last], axis=1).astype(bf16)
    for z in range(8):
        out[z] = full


def copies_body(x_ref, out):
    for e in range(16):
        out[e] = x_ref[...]


def logit_body(tokens, cot, lt_ref, gm, gt, r_mine, r_theirs, dl_ref, w_ref, g_ref, r_sum):
    grad = is_grad_row((256, TOK))
    grad_half = is_grad_row((256, 640))
    halves = [
        [
            jnp.concatenate([g[8 * yl + j].astype(f32).reshape(64, PART) for yl in range(2)], axis=0)
            for j in range(8)
        ]
        for g in (gm, gt)
    ]
    dots = [functools.reduce(jnp.add, [part[:, 384:] for part in h]) for h in halves]
    dots = join_triple(jnp.concatenate(dots, axis=0))
    stats = join_triple(jnp.concatenate([h[0][:, 384:] for h in halves], axis=0))
    stats = pltpu.roll(stats, 4, 0)
    for c in range(CLIPS):
        low = jnp.concatenate([rows_of(h, c).astype(bf16) for h in halves], axis=0)
        g_ref[c] = low
        at = STAT + 8 * c
        peak = stats[:, at : at + 1]
        total = stats[:, at + 3 : at + 4]
        column_dot = dots[:, at : at + 1]
        logits = lt_ref[c]
        raised = jnp.exp(logits - jnp.max(logits, axis=0, keepdims=True))
        combine = raised * (2.0 / jnp.sum(raised, axis=0, keepdims=True))
        combine = jnp.where(grad, 0.0, combine)
        d_combine = dot(low, cot[c], NT)
        inner = jnp.sum(combine * d_combine, axis=0, keepdims=True)
        dispatch = jnp.where(grad, jnp.exp(logits - peak) * (1.0 / total), 0.0)
        d_dispatch = dot(low, tokens[c], NT)
        own = jnp.where(grad, dispatch * (d_dispatch - column_dot), combine * (d_combine - inner))
        d_logit = (own + swap_halves(own, grad)).astype(bf16)
        part = dot(d_logit, tokens[c])
        part = jnp.where(grad_half, part[:, 640:], part[:, :640])
        if c == 0:
            r_sum[...] = part
        else:
            r_sum[...] += part
        dl_ref[c] = jnp.where(grad, 0.0, d_logit.astype(f32)).astype(bf16)
        w_ref[c] = dispatch.astype(bf16)
    r_mine[...] = r_sum[:128].astype(bf16).reshape(16, 8, 640)
    r_theirs[...] = r_sum[128:].astype(bf16).reshape(16, 8, 640)


def tokens_body(clips, dl_ref, w_ref, rt_ref, g_ref, *rest):
    out, buffer, sems = rest[-3:]
    copies = []
    for c in clips:
        tile = dot(dl_ref[c], rt_ref[...], TN) + dot(w_ref[c], g_ref[c], TN)
        buffer[c] = tile.astype(bf16)
        copies.append(pltpu.make_async_copy(buffer.at[c], out.at[c], sems.at[c]))
        copies[-1].start()
    for copy in copies:
        copy.wait()


def token_clips(clips, *args):
    local = (CLIPS, TOK, D)
    return pl.pallas_call(
        functools.partial(tokens_body, clips),
        out_shape=jax.ShapeDtypeStruct(local, bf16),
        in_specs=[pl.BlockSpec(memory_space=pltpu.VMEM)] * 4
        + [pl.BlockSpec(memory_space=pltpu.HBM)] * (len(args) - 4),
        out_specs=pl.BlockSpec(memory_space=pltpu.HBM),
        scratch_shapes=[pltpu.VMEM(local, bf16), pltpu.SemaphoreType.DMA((CLIPS,))],
        input_output_aliases={4: 0} if len(args) > 4 else {},
        compiler_params=pltpu.CompilerParams(vmem_limit_bytes=16 * MiB),
        cost_estimate=pl.CostEstimate(flops=10**9, bytes_accessed=3 * 10**6, transcendentals=0),
    )(*args)


def add_body(a_ref, b_ref, out):
    out[...] = (a_ref[...].astype(f32) + b_ref[...].astype(f32)).astype(bf16)


def spread_body(x_ref, out):
    acc = x_ref[0].astype(f32)
    for i in range(1, x_ref.shape[0]):
        acc = acc + x_ref[i].astype(f32)
    acc = acc.astype(bf16)
    for i in range(out.shape[0]):
        out[i] = acc


def router_body(core_ref, mine, theirs, out):
    hit, t = slot_of_row(core_ref[0])
    rows = [x[...].astype(f32).reshape(128, 640) for x in (mine, theirs)]
    rows = jnp.concatenate(rows, axis=0).astype(bf16)
    for a in range(2):
        pick = (hit & ((t % 8) // 4 == a)).astype(f32).astype(bf16)
        out[a * 640 : (a + 1) * 640, :] = dot(rows, pick, TN)


def exchange(x, axes):
    return lax.all_to_all(x, axes, 0, 0, tiled=True)


def to_partner(x):
    return lax.ppermute(x, "core", [(0, 1), (1, 0)])


def per_device(tokens, router, w_in, w_out, cotangent):
    core = lax.axis_index("core").astype(jnp.int32).reshape(1)
    values = ((8, 16, 8, PART), bf16)
    planes = ((16, 8, 8, PART), bf16)
    local = (CLIPS, TOK, D)
    square = ((CLIPS, 256, TOK), bf16)
    mine, theirs, rt, lt = call(
        slots_body,
        [(values[0], f32), values, ((256, D), bf16), ((CLIPS, 256, TOK), f32)],
        core,
        *[pltpu.with_memory_space_constraint(x, pltpu.HBM) for x in (router, tokens, cotangent)],
        scratch=[
            pltpu.VMEM((D, 128), bf16),
            pltpu.VMEM(local, bf16),
            pltpu.VMEM(local, bf16),
            pltpu.VMEM(*square),
            pltpu.VMEM(*square),
            pltpu.SemaphoreType.DMA((2, CLIPS)),
            pltpu.SemaphoreType.DMA,
        ],
        smem=(0,),
        hbm=(1, 2, 3),
        flops=3 * 10**9,
        nbytes=8 * 10**6,
        limit=24,
    )
    (sums,) = call(pair_body, [planes], mine, to_partner(theirs), flops=10**10, nbytes=3 * 10**6)
    (sums,) = call(
        members_body, [((8, 8, PART), f32)], exchange(sums, PLANE), flops=10**10, nbytes=10**6
    )
    sums, own = call(
        owner_body,
        [((8, 8, PART), bf16), ((8, PART), f32)],
        exchange(sums, ("z",)),
        nbytes=10**5,
    )
    parts, stats = call(
        expert_body,
        [((8, 8, PART), f32), ((8, 128), f32)],
        exchange(sums, EXP),
        w_in,
        w_out,
        flops=10**9,
        nbytes=8 * 10**6,
    )
    (result,) = call(
        result_body, [((8, 8, PART), bf16)], exchange(parts, EXP), stats, own, nbytes=10**5
    )
    (result,) = call(copies_body, [planes], exchange(result, ("z",)), nbytes=10**6)
    g_mine = exchange(result, PLANE)
    g_theirs = to_partner(g_mine)
    half = ((16, 8, 640), bf16)
    r_mine, r_theirs, d_logit, dispatch, grads = call(
        logit_body,
        [half, half, square, square, (local, bf16)],
        tokens,
        cotangent,
        lt,
        g_mine,
        g_theirs,
        scratch=[pltpu.VMEM((256, 640), f32)],
        flops=3 * 10**9,
        nbytes=10**7,
        limit=24,
    )
    work = (d_logit, dispatch, rt, grads)
    got, d_tokens = lax.optimization_barrier((to_partner(r_theirs), token_clips((0,), *work)))
    (r_mine,) = call(add_body, [half], r_mine, got, nbytes=10**6)
    d_tokens = token_clips((1, 2), *work, d_tokens)
    r_mine = exchange(r_mine, PLANE)
    (r_mine,) = call(spread_body, [((8, 8, 640), bf16)], r_mine, nbytes=10**5)
    r_mine = exchange(r_mine, ("z",))
    (r_mine,) = call(spread_body, [half], r_mine, nbytes=10**5)
    r_mine = exchange(r_mine, PLANE)
    (d_router,) = call(
        router_body, [((D, 128), f32)], core, r_mine, to_partner(r_mine), smem=(0,), nbytes=2 * 10**6
    )
    return (d_tokens, d_router)


def solution(mesh):
    fine = Mesh(mesh.devices.reshape(tuple(SIZES.values())), AXES)
    seq = ("yl", "z", "core")
    placed = (
        P(None, AXES, None),
        P(),
        P(seq, None, EXP),
        P(seq, EXP, None),
        P(None, AXES, None),
    )
    return jax.shard_map(
        per_device,
        mesh=fine,
        in_specs=placed,
        out_specs=(P(None, AXES, None), P()),
        check_vma=False,
    )
```

```python
import functools

import jax
import jax.numpy as jnp
from jax import lax
from jax.experimental import pallas as pl
from jax.experimental.pallas import tpu as pltpu
from jax.sharding import Mesh, PartitionSpec as P

SIZES = {"yl": 2, "z": 8, "core": 2, "yh": 2, "x": 4}
AXES = tuple(SIZES)
EXP = ("yh", "x")
PLANE = ("yl", "yh", "x")

D = 1280
CLIPS = 3
TOK = 256
ROWS = 24
PART = 512
STAT = 96
MiB = 1024 * 1024
GELU_C = 0.7978845608028654
GELU_A = 0.044715

bf16 = jnp.bfloat16
f32 = jnp.float32

NT = (((1,), (1,)), ((), ()))
TN = (((0,), (0,)), ((), ()))


def dot(a, b, dims=None):
    if dims is None:
        return jnp.dot(a, b, preferred_element_type=f32)
    return lax.dot_general(a, b, dims, preferred_element_type=f32)


def is_grad_row(shape):
    return lax.broadcasted_iota(jnp.int32, shape, 0) % 8 >= 4


def swap_halves(v, grad):
    n = v.shape[0]
    return jnp.where(grad, pltpu.roll(v, 4, 0), pltpu.roll(v, n - 4, 0))


def lanes_of(shape):
    return lax.broadcasted_iota(jnp.int32, shape, len(shape) - 1)


def split(value):
    high = value.astype(bf16).astype(f32)
    rest = value - high
    middle = rest.astype(bf16).astype(f32)
    return high, middle, rest - middle


def spread_triple(value):
    high, middle, low = split(value)
    return high + pltpu.roll(middle, 1, 1) + pltpu.roll(low, 2, 1)


def join_triple(stats):
    return stats + pltpu.roll(stats, 127, 1) + pltpu.roll(stats, 126, 1)


def clip_columns(x):
    return [x[:, STAT + 8 * c : STAT + 8 * c + 1] for c in range(CLIPS)]


def by_quarter(columns, lane):
    first = jnp.where(lane < 32, columns[0], columns[1])
    return jnp.where(lane < 64, first, columns[2])


def merge_stats(last):
    joined = [join_triple(x) for x in last]
    peak = functools.reduce(jnp.maximum, joined)
    scales = [jnp.exp(jnp.minimum(j - peak, 0.0)) for j in joined]
    total = functools.reduce(jnp.add, [pltpu.roll(x, 3, 1) * j for x, j in zip(scales, joined)])
    lane = lanes_of(peak.shape)
    stats = jnp.where(lane % 8 == 0, peak, jnp.where(lane % 8 == 3, total, 0.0))
    stats = spread_triple(jnp.where(lane < STAT, 0.0, stats))
    return [clip_columns(x) for x in scales], stats


def merge_tiles(wide, columns, stats):
    tiles = []
    for c in range(CLIPS):
        lanes = slice(128 * c, 128 * c + 128)
        parts = [col[c] * b[:, lanes] for b, col in zip(wide, columns)]
        tiles.append(functools.reduce(jnp.add, parts))
    lane = lanes_of(stats.shape)
    parts = [by_quarter(col, lane) * b[:, 384:] for b, col in zip(wide, columns)]
    tiles.append(jnp.where(lane < STAT, functools.reduce(jnp.add, parts), stats))
    return jnp.concatenate(tiles, axis=1)


def merge_blocks(blocks):
    wide = [b.astype(f32) for b in blocks]
    return merge_tiles(wide, *merge_stats([b[:, 384:] for b in wide]))


def rows_of(blocks, c):
    lane = lanes_of((blocks[0].shape[0], 128))
    tiles = [b[:, 128 * c : 128 * c + 128] for b in blocks]
    for first in (0, 4):
        tile = None
        for q in range(4):
            turned = blocks[first + q][:, 384:]
            if q != c:
                turned = pltpu.roll(turned, 32 * (q - c) % 128, 1)
            tile = turned if tile is None else jnp.where(lane // 32 == q, turned, tile)
        tiles.append(tile)
    return jnp.concatenate(tiles, axis=1)


def last_tile(tails, j, stats):
    lane = lanes_of(stats.shape)
    out = stats
    for c, tail in enumerate(tails):
        tile = tail[:, 128 * (j // 4) : 128 * (j // 4) + 128]
        if j % 4 != c:
            tile = pltpu.roll(tile, 32 * (c - j % 4) % 128, 1)
        out = jnp.where(lane // 32 == c, tile, out)
    return out


def call(body, outs, *args, scratch=(), flops=0, nbytes=0, smem=(), hbm=(), limit=16):
    spaces = [
        pltpu.SMEM if i in smem else pltpu.HBM if i in hbm else pltpu.VMEM for i in range(len(args))
    ]
    return pl.pallas_call(
        body,
        out_shape=[jax.ShapeDtypeStruct(s, t) for s, t in outs],
        in_specs=[pl.BlockSpec(memory_space=s) for s in spaces],
        out_specs=[pl.BlockSpec(memory_space=pltpu.VMEM) for _ in outs],
        scratch_shapes=list(scratch),
        compiler_params=pltpu.CompilerParams(vmem_limit_bytes=limit * MiB),
        cost_estimate=pl.CostEstimate(flops=flops, bytes_accessed=nbytes, transcendentals=0),
    )(*args)


def slot_of_row(core):
    t = lax.broadcasted_iota(jnp.int32, (256, 128), 0)
    s = lax.broadcasted_iota(jnp.int32, (256, 128), 1)
    half = t // 128
    slot = 8 * ((t % 128) // 8) + 4 * (half + core * (1 - 2 * half)) + t % 4
    return s == slot, t


def fill_parts(out, weights_in, weights_out, tokens, cot, stats, before=None):
    def product(c, lanes):
        return dot(weights_in[c], tokens[c, :, lanes]) + dot(weights_out[c], cot[c, :, lanes])

    for c in range(CLIPS):
        if before is not None:
            before[c].wait()
        for i in range(4):
            part = product(c, slice(256 * i, 256 * i + 256)).reshape(16, 8, 256)
            for h in range(2):
                tile = part[:, :, 128 * h : 128 * h + 128]
                out[2 * i + h, :, :, 128 * c : 128 * c + 128] = tile.astype(out.dtype)
    tails = [product(c, slice(1024, 1280)) for c in range(CLIPS)]
    for j in range(8):
        out[j, :, :, 384:] = last_tile(tails, j, stats).reshape(16, 8, 128).astype(out.dtype)


def slots_body(
    core_ref, router_hbm, tokens_hbm, cot_hbm, theirs, rt_ref, lt_ref, tokens, cot,
    own_in, own_out, own_stats, router, weights_in, weights_out, sems, router_sem,
):
    first = pltpu.make_async_copy(router_hbm, router, router_sem)
    copies = [
        pltpu.make_async_copy(src.at[c], dst.at[c], sems.at[i, c])
        for i, (src, dst) in enumerate(((tokens_hbm, tokens), (cot_hbm, cot)))
        for c in range(CLIPS)
    ]
    first.start()
    copies[0].start()
    pick, _ = slot_of_row(core_ref[0])
    pick = pick.astype(f32).astype(bf16)
    first.wait()
    copies[1].start()
    rt_ref[...] = dot(pick, router[...], NT).astype(bf16)
    grad = is_grad_row((256, TOK))
    lane = lanes_of((256, 128))
    stats = jnp.zeros((256, 128), f32)
    for c in range(CLIPS):
        copies[c].wait()
        for copy in copies[2 * c + 2 : min(2 * c + 4, 6)]:
            copy.start()
        logits = dot(rt_ref[...], tokens[c], NT)
        lt_ref[c] = logits
        peak = jnp.max(logits, axis=1, keepdims=True)
        low = jnp.where(grad, 0.0, jnp.exp(logits - peak)).astype(bf16)
        total = jnp.sum(low.astype(f32), axis=1, keepdims=True)
        own_in[c] = low[:128]
        weights_in[c] = low[128:]
        raised = jnp.exp(logits - jnp.max(logits, axis=0, keepdims=True))
        combine = raised * (2.0 / jnp.sum(raised, axis=0, keepdims=True))
        combine = jnp.where(grad, combine, 0.0).astype(bf16)
        own_out[c] = combine[:128]
        weights_out[c] = combine[128:]
        at = STAT + 8 * c
        stats = jnp.where(lane == at, peak, jnp.where(lane == at + 3, total, stats))
    ones = jnp.where((lane >= STAT) & (lane % 8 == 3), 1.0, 0.0)
    stats = spread_triple(jnp.where(is_grad_row((256, 128)), ones, stats))
    own_stats[...] = stats[:128]
    fill_parts(theirs, weights_in, weights_out, tokens, cot, stats[128:], copies[CLIPS:])


def own_body(own_in, own_out, own_stats, tokens, cot, mine):
    fill_parts(mine, own_in, own_out, tokens, cot, own_stats[...])


def pair_body(a_ref, b_ref, out):
    columns, stats = merge_stats([x[0, :, :, 384:].astype(f32).reshape(128, 128) for x in (a_ref, b_ref)])
    for j in range(8):
        wide = [x[j].astype(f32).reshape(128, PART) for x in (a_ref, b_ref)]
        merged = merge_tiles(wide, columns, stats).astype(bf16)
        out[j] = merged[:64].reshape(8, 8, PART)
        out[8 + j] = merged[64:].reshape(8, 8, PART)


def members_body(x_ref, out):
    blocks = [x_ref[e].astype(f32).reshape(64, PART) for e in range(16)]
    out[...] = merge_blocks(blocks).reshape(8, 8, PART)


def owner_body(x_ref, out, own):
    merged = merge_blocks([x_ref[z] for z in range(8)])
    last = merged[:, 384:]
    joined = join_triple(last)
    grad = is_grad_row((8, 1))
    totals = [joined[:, STAT + 8 * c + 3 : STAT + 8 * c + 4] for c in range(CLIPS)]
    inverse = [jnp.where(grad, 1.0, 1.0 / total) for total in totals]
    lane = lanes_of(last.shape)
    tiles = [merged[:, 128 * c : 128 * c + 128] * inverse[c] for c in range(CLIPS)]
    tiles.append(jnp.where(lane < STAT, last * by_quarter(inverse, lane), last))
    rows = jnp.concatenate(tiles, axis=1)
    own[...] = rows
    low = rows.astype(bf16)
    for e in range(8):
        out[e] = low


def gelu_parts(v):
    t = jnp.tanh(GELU_C * (v + GELU_A * (v * v * v)))
    value = 0.5 * v * (1.0 + t)
    slope = 0.5 * (1.0 + t) + 0.5 * v * (1.0 - t * t) * (GELU_C * (1.0 + 3.0 * GELU_A * (v * v)))
    return value, slope


def expert_body(x_ref, w_in, w_out, out, stats_out):
    blocks = [x_ref[e].astype(f32) for e in range(8)]
    stats_out[...] = join_triple(blocks[0][:, 384:])
    low = jnp.concatenate([rows_of(blocks, c) for c in range(CLIPS)], axis=0).astype(bf16)
    row = lax.broadcasted_iota(jnp.int32, (ROWS, 640), 0)
    grad = row % 8 >= 4
    acc = jnp.zeros((ROWS, D), f32)
    for i in range(2):
        own = (row % 4) // 2 == i
        value, slope = gelu_parts(dot(low, w_in[i]))
        d_pre = dot(low, w_out[i], NT) * pltpu.roll(slope, 4, 0)
        hidden = jnp.where(own & jnp.logical_not(grad), value, 0.0).astype(bf16)
        d_pre = jnp.where(own & grad, d_pre, 0.0).astype(bf16)
        acc = acc + dot(hidden, w_out[i]) + dot(d_pre, w_in[i], NT)
    by_clip = [acc[8 * c : 8 * c + 8] for c in range(CLIPS)]
    tails = [rows[:, 1024:] for rows in by_clip]
    empty = jnp.zeros((8, 128), f32)
    for j in range(8):
        tiles = [rows[:, 128 * j : 128 * j + 128] for rows in by_clip]
        out[j] = jnp.concatenate(tiles + [last_tile(tails, j, empty)], axis=1)


def result_body(x_ref, joined, own, out):
    acc = x_ref[0]
    for e in range(1, 8):
        acc = acc + x_ref[e]
    low = acc.astype(bf16).astype(f32)
    products = low * pltpu.roll(own[...], 4, 0)
    lane = lanes_of((8, 128))
    grad = is_grad_row((8, 128))
    kept = jnp.where((lane % 8 == 0) | (lane % 8 == 3), joined[...], 0.0)
    dots = jnp.zeros((8, 128), f32)
    for c in range(CLIPS):
        both = products[:, 128 * c : 128 * c + 128]
        both = both + jnp.where(lane // 32 == c, products[:, 384:], 0.0)
        total = jnp.sum(both, axis=1, keepdims=True)
        dots = jnp.where(lane == STAT + 8 * c, total, dots)
    stats = spread_triple(jnp.where(lane < STAT, 0.0, jnp.where(grad, dots, kept)))
    last = jnp.where(lane < STAT, low[:, 384:], stats)
    full = jnp.concatenate([low[:, :384], last], axis=1).astype(bf16)
    for z in range(8):
        out[z] = full


def copies_body(x_ref, out):
    for e in range(16):
        out[e] = x_ref[...]


def half_of(g, tokens, cot, low_ref):
    blocks = [
        jnp.concatenate([g[8 * yl + j].astype(f32).reshape(64, PART) for yl in range(2)], axis=0)
        for j in range(8)
    ]
    dots = functools.reduce(jnp.add, [part[:, 384:] for part in blocks])
    d_combine, d_dispatch = [], []
    for c in range(CLIPS):
        low = rows_of(blocks, c).astype(bf16)
        low_ref[c] = low
        d_combine.append(dot(low, cot[c], NT))
        d_dispatch.append(dot(low, tokens[c], NT))
    return d_combine, d_dispatch, join_triple(dots), join_triple(blocks[0][:, 384:])


def near_body(tokens, cot, g, low_ref, dc_ref, dd_ref, dots_ref, stats_ref):
    d_combine, d_dispatch, dots, stats = half_of(g, tokens, cot, low_ref)
    for c in range(CLIPS):
        dc_ref[c] = d_combine[c]
        dd_ref[c] = d_dispatch[c]
    dots_ref[...] = dots
    stats_ref[...] = stats


def logit_body(
    tokens, cot, lt_ref, dc_ref, dd_ref, dots_ref, stats_ref, g,
    r_mine, r_theirs, dl_ref, w_ref, low_ref, r_sum,
):
    grad = is_grad_row((256, TOK))
    grad_half = is_grad_row((256, 640))
    far_combine, far_dispatch, far_dots, far_stats = half_of(g, tokens, cot, low_ref)
    dots = jnp.concatenate([dots_ref[...], far_dots], axis=0)
    stats = pltpu.roll(jnp.concatenate([stats_ref[...], far_stats], axis=0), 4, 0)
    for c in range(CLIPS):
        at = STAT + 8 * c
        peak = stats[:, at : at + 1]
        total = stats[:, at + 3 : at + 4]
        column_dot = dots[:, at : at + 1]
        logits = lt_ref[c]
        raised = jnp.exp(logits - jnp.max(logits, axis=0, keepdims=True))
        combine = raised * (2.0 / jnp.sum(raised, axis=0, keepdims=True))
        combine = jnp.where(grad, 0.0, combine)
        d_combine = jnp.concatenate([dc_ref[c], far_combine[c]], axis=0)
        inner = jnp.sum(combine * d_combine, axis=0, keepdims=True)
        dispatch = jnp.where(grad, jnp.exp(logits - peak) * (1.0 / total), 0.0)
        d_dispatch = jnp.concatenate([dd_ref[c], far_dispatch[c]], axis=0)
        own = jnp.where(grad, dispatch * (d_dispatch - column_dot), combine * (d_combine - inner))
        d_logit = (own + swap_halves(own, grad)).astype(bf16)
        part = dot(d_logit, tokens[c])
        part = jnp.where(grad_half, part[:, 640:], part[:, :640])
        if c == 0:
            r_sum[...] = part
        else:
            r_sum[...] += part
        dl_ref[c] = jnp.where(grad, 0.0, d_logit.astype(f32)).astype(bf16)
        w_ref[c] = dispatch.astype(bf16)
    r_mine[...] = r_sum[:128].astype(bf16).reshape(16, 8, 640)
    r_theirs[...] = r_sum[128:].astype(bf16).reshape(16, 8, 640)


def tokens_body(clips, dl_ref, w_ref, rt_ref, near_ref, far_ref, *rest):
    out, buffer, sems = rest[-3:]
    copies = []
    for c in clips:
        rows = jnp.concatenate([near_ref[c], far_ref[c]], axis=0)
        tile = dot(dl_ref[c], rt_ref[...], TN) + dot(w_ref[c], rows, TN)
        buffer[c] = tile.astype(bf16)
        copies.append(pltpu.make_async_copy(buffer.at[c], out.at[c], sems.at[c]))
        copies[-1].start()
    for copy in copies:
        copy.wait()


def token_clips(clips, *args):
    local = (CLIPS, TOK, D)
    return pl.pallas_call(
        functools.partial(tokens_body, clips),
        out_shape=jax.ShapeDtypeStruct(local, bf16),
        in_specs=[pl.BlockSpec(memory_space=pltpu.VMEM)] * 5
        + [pl.BlockSpec(memory_space=pltpu.HBM)] * (len(args) - 5),
        out_specs=pl.BlockSpec(memory_space=pltpu.HBM),
        scratch_shapes=[pltpu.VMEM(local, bf16), pltpu.SemaphoreType.DMA((CLIPS,))],
        input_output_aliases={5: 0} if len(args) > 5 else {},
        compiler_params=pltpu.CompilerParams(vmem_limit_bytes=16 * MiB),
        cost_estimate=pl.CostEstimate(flops=10**9, bytes_accessed=3 * 10**6, transcendentals=0),
    )(*args)


def add_body(a_ref, b_ref, out):
    out[...] = (a_ref[...].astype(f32) + b_ref[...].astype(f32)).astype(bf16)


def spread_body(x_ref, out):
    acc = x_ref[0].astype(f32)
    for i in range(1, x_ref.shape[0]):
        acc = acc + x_ref[i].astype(f32)
    acc = acc.astype(bf16)
    for i in range(out.shape[0]):
        out[i] = acc


def router_body(core_ref, mine, theirs, out):
    hit, t = slot_of_row(core_ref[0])
    rows = [x[...].astype(f32).reshape(128, 640) for x in (mine, theirs)]
    rows = jnp.concatenate(rows, axis=0).astype(bf16)
    for a in range(2):
        pick = (hit & ((t % 8) // 4 == a)).astype(f32).astype(bf16)
        out[a * 640 : (a + 1) * 640, :] = dot(rows, pick, TN)


def exchange(x, axes):
    return lax.all_to_all(x, axes, 0, 0, tiled=True)


def to_partner(x):
    return lax.ppermute(x, "core", [(0, 1), (1, 0)])


def per_device(tokens, router, w_in, w_out, cotangent):
    core = lax.axis_index("core").astype(jnp.int32).reshape(1)
    values = ((8, 16, 8, PART), bf16)
    planes = ((16, 8, 8, PART), bf16)
    local = (CLIPS, TOK, D)
    square = ((CLIPS, 256, TOK), bf16)
    own = ((CLIPS, 128, TOK), bf16)
    theirs, rt, lt, tokens, cotangent, own_in, own_out, own_stats = call(
        slots_body,
        [
            values,
            ((256, D), bf16),
            ((CLIPS, 256, TOK), f32),
            (local, bf16),
            (local, bf16),
            own,
            own,
            ((128, 128), f32),
        ],
        core,
        *[pltpu.with_memory_space_constraint(x, pltpu.HBM) for x in (router, tokens, cotangent)],
        scratch=[
            pltpu.VMEM((D, 128), bf16),
            pltpu.VMEM(*own),
            pltpu.VMEM(*own),
            pltpu.SemaphoreType.DMA((2, CLIPS)),
            pltpu.SemaphoreType.DMA,
        ],
        smem=(0,),
        hbm=(1, 2, 3),
        flops=3 * 10**9,
        nbytes=8 * 10**6,
        limit=24,
    )
    (mine,) = call(
        own_body,
        [(values[0], f32)],
        own_in,
        own_out,
        own_stats,
        tokens,
        cotangent,
        flops=10**9,
        nbytes=8 * 10**6,
        limit=24,
    )
    (sums,) = call(pair_body, [planes], mine, to_partner(theirs), flops=10**10, nbytes=3 * 10**6)
    (sums,) = call(
        members_body, [((8, 8, PART), f32)], exchange(sums, PLANE), flops=10**10, nbytes=10**6
    )
    sums, own = call(
        owner_body,
        [((8, 8, PART), bf16), ((8, PART), f32)],
        exchange(sums, ("z",)),
        nbytes=10**5,
    )
    parts, stats = call(
        expert_body,
        [((8, 8, PART), f32), ((8, 128), f32)],
        exchange(sums, EXP),
        w_in,
        w_out,
        flops=10**9,
        nbytes=8 * 10**6,
    )
    (result,) = call(
        result_body, [((8, 8, PART), bf16)], exchange(parts, EXP), stats, own, nbytes=10**5
    )
    (result,) = call(copies_body, [planes], exchange(result, ("z",)), nbytes=10**6)
    g_mine = exchange(result, PLANE)
    g_theirs = to_partner(g_mine)
    half = ((16, 8, 640), bf16)
    pair = ((CLIPS, 128, TOK), f32)
    near, d_combine, d_dispatch, dots, stats = call(
        near_body,
        [((CLIPS, 128, D), bf16), pair, pair, ((128, 128), f32), ((128, 128), f32)],
        tokens,
        cotangent,
        g_mine,
        flops=10**9,
        nbytes=6 * 10**6,
    )
    r_mine, r_theirs, d_logit, dispatch, far = call(
        logit_body,
        [half, half, square, square, ((CLIPS, 128, D), bf16)],
        tokens,
        cotangent,
        lt,
        d_combine,
        d_dispatch,
        dots,
        stats,
        g_theirs,
        scratch=[pltpu.VMEM((256, 640), f32)],
        flops=3 * 10**9,
        nbytes=10**7,
        limit=24,
    )
    work = (d_logit, dispatch, rt, near, far)
    got, d_tokens = lax.optimization_barrier((to_partner(r_theirs), token_clips((0,), *work)))
    (r_mine,) = call(add_body, [half], r_mine, got, nbytes=10**6)
    d_tokens = token_clips((1, 2), *work, d_tokens)
    r_mine = exchange(r_mine, PLANE)
    (r_mine,) = call(spread_body, [((8, 8, 640), bf16)], r_mine, nbytes=10**5)
    r_mine = exchange(r_mine, ("z",))
    (r_mine,) = call(spread_body, [half], r_mine, nbytes=10**5)
    r_mine = exchange(r_mine, PLANE)
    (d_router,) = call(
        router_body, [((D, 128), f32)], core, r_mine, to_partner(r_mine), smem=(0,), nbytes=2 * 10**6
    )
    return (d_tokens, d_router)


def solution(mesh):
    fine = Mesh(mesh.devices.reshape(tuple(SIZES.values())), AXES)
    seq = ("yl", "z", "core")
    placed = (
        P(None, AXES, None),
        P(),
        P(seq, None, EXP),
        P(seq, EXP, None),
        P(None, AXES, None),
    )
    return jax.shard_map(
        per_device,
        mesh=fine,
        in_specs=placed,
        out_specs=(P(None, AXES, None), P()),
        check_vma=False,
    )
```

```python
import functools

import jax
import jax.numpy as jnp
from jax import lax
from jax.experimental import pallas as pl
from jax.experimental.pallas import tpu as pltpu
from jax.sharding import Mesh, PartitionSpec as P

SIZES = {"yl": 2, "z": 8, "core": 2, "yh": 2, "x": 4}
AXES = tuple(SIZES)
EXP = ("yh", "x")
PLANE = ("yl", "yh", "x")

D = 1280
CLIPS = 3
TOK = 256
ROWS = 24
PART = 512
STAT = 96
MiB = 1024 * 1024
GELU_C = 0.7978845608028654
GELU_A = 0.044715

bf16 = jnp.bfloat16
f32 = jnp.float32

NT = (((1,), (1,)), ((), ()))
TN = (((0,), (0,)), ((), ()))


def dot(a, b, dims=None):
    if dims is None:
        return jnp.dot(a, b, preferred_element_type=f32)
    return lax.dot_general(a, b, dims, preferred_element_type=f32)


def is_grad_row(shape):
    return lax.broadcasted_iota(jnp.int32, shape, 0) % 8 >= 4


def swap_halves(v, grad):
    n = v.shape[0]
    return jnp.where(grad, pltpu.roll(v, 4, 0), pltpu.roll(v, n - 4, 0))


def lanes_of(shape):
    return lax.broadcasted_iota(jnp.int32, shape, len(shape) - 1)


def split(value):
    high = value.astype(bf16).astype(f32)
    rest = value - high
    middle = rest.astype(bf16).astype(f32)
    return high, middle, rest - middle


def spread_triple(value):
    high, middle, low = split(value)
    return high + pltpu.roll(middle, 1, 1) + pltpu.roll(low, 2, 1)


def join_triple(stats):
    return stats + pltpu.roll(stats, 127, 1) + pltpu.roll(stats, 126, 1)


def clip_columns(x):
    return [x[:, STAT + 8 * c : STAT + 8 * c + 1] for c in range(CLIPS)]


def by_quarter(columns, lane):
    first = jnp.where(lane < 32, columns[0], columns[1])
    return jnp.where(lane < 64, first, columns[2])


def merge_stats(last):
    joined = [join_triple(x) for x in last]
    peak = functools.reduce(jnp.maximum, joined)
    scales = [jnp.exp(jnp.minimum(j - peak, 0.0)) for j in joined]
    total = functools.reduce(jnp.add, [pltpu.roll(x, 3, 1) * j for x, j in zip(scales, joined)])
    lane = lanes_of(peak.shape)
    stats = jnp.where(lane % 8 == 0, peak, jnp.where(lane % 8 == 3, total, 0.0))
    stats = spread_triple(jnp.where(lane < STAT, 0.0, stats))
    return [clip_columns(x) for x in scales], stats


def merge_tiles(wide, columns, stats):
    tiles = []
    for c in range(CLIPS):
        lanes = slice(128 * c, 128 * c + 128)
        parts = [col[c] * b[:, lanes] for b, col in zip(wide, columns)]
        tiles.append(functools.reduce(jnp.add, parts))
    lane = lanes_of(stats.shape)
    parts = [by_quarter(col, lane) * b[:, 384:] for b, col in zip(wide, columns)]
    tiles.append(jnp.where(lane < STAT, functools.reduce(jnp.add, parts), stats))
    return jnp.concatenate(tiles, axis=1)


def merge_blocks(blocks):
    wide = [b.astype(f32) for b in blocks]
    return merge_tiles(wide, *merge_stats([b[:, 384:] for b in wide]))


def rows_of(blocks, c):
    lane = lanes_of((blocks[0].shape[0], 128))
    tiles = [b[:, 128 * c : 128 * c + 128] for b in blocks]
    for first in (0, 4):
        tile = None
        for q in range(4):
            turned = blocks[first + q][:, 384:]
            if q != c:
                turned = pltpu.roll(turned, 32 * (q - c) % 128, 1)
            tile = turned if tile is None else jnp.where(lane // 32 == q, turned, tile)
        tiles.append(tile)
    return jnp.concatenate(tiles, axis=1)


def last_tile(tails, j, stats):
    lane = lanes_of(stats.shape)
    out = stats
    for c, tail in enumerate(tails):
        tile = tail[:, 128 * (j // 4) : 128 * (j // 4) + 128]
        if j % 4 != c:
            tile = pltpu.roll(tile, 32 * (c - j % 4) % 128, 1)
        out = jnp.where(lane // 32 == c, tile, out)
    return out


def call(body, outs, *args, scratch=(), flops=0, nbytes=0, smem=(), hbm=(), limit=16):
    spaces = [
        pltpu.SMEM if i in smem else pltpu.HBM if i in hbm else pltpu.VMEM for i in range(len(args))
    ]
    return pl.pallas_call(
        body,
        out_shape=[jax.ShapeDtypeStruct(s, t) for s, t in outs],
        in_specs=[pl.BlockSpec(memory_space=s) for s in spaces],
        out_specs=[pl.BlockSpec(memory_space=pltpu.VMEM) for _ in outs],
        scratch_shapes=list(scratch),
        compiler_params=pltpu.CompilerParams(vmem_limit_bytes=limit * MiB),
        cost_estimate=pl.CostEstimate(flops=flops, bytes_accessed=nbytes, transcendentals=0),
    )(*args)


def slot_of_row(core):
    t = lax.broadcasted_iota(jnp.int32, (256, 128), 0)
    s = lax.broadcasted_iota(jnp.int32, (256, 128), 1)
    half = t // 128
    slot = 8 * ((t % 128) // 8) + 4 * (half + core * (1 - 2 * half)) + t % 4
    return s == slot, t


def fill_parts(out, weights_in, weights_out, tokens, cot, stats, before=None):
    def product(c, lanes):
        return dot(weights_in[c], tokens[c, :, lanes]) + dot(weights_out[c], cot[c, :, lanes])

    for c in range(CLIPS):
        if before is not None:
            before[c].wait()
        for i in range(4):
            part = product(c, slice(256 * i, 256 * i + 256)).reshape(16, 8, 256)
            for h in range(2):
                tile = part[:, :, 128 * h : 128 * h + 128]
                out[2 * i + h, :, :, 128 * c : 128 * c + 128] = tile.astype(out.dtype)
    tails = [product(c, slice(1024, 1280)) for c in range(CLIPS)]
    for j in range(8):
        out[j, :, :, 384:] = last_tile(tails, j, stats).reshape(16, 8, 128).astype(out.dtype)


def slots_body(
    core_ref, router_hbm, tokens_hbm, cot_hbm, theirs, rt_ref, lt_ref, tokens, cot,
    own_in, own_out, own_stats, router, weights_in, weights_out, sems, router_sem,
):
    first = pltpu.make_async_copy(router_hbm, router, router_sem)
    copies = [
        pltpu.make_async_copy(src.at[c], dst.at[c], sems.at[i, c])
        for i, (src, dst) in enumerate(((tokens_hbm, tokens), (cot_hbm, cot)))
        for c in range(CLIPS)
    ]
    first.start()
    copies[0].start()
    copies[1].start()
    row = lax.broadcasted_iota(jnp.int32, (128, 128), 0)
    lane = lanes_of((128, 128))
    same = (row == lane).astype(f32).astype(bf16)
    first.wait()
    rt_ref[...] = dot(same, router[...], NT).astype(bf16)
    low_core = core_ref[0] == 0
    grad = is_grad_row((128, TOK))
    stats = jnp.zeros((128, 128), f32)
    for c in range(CLIPS):
        copies[c].wait()
        for copy in copies[2 * c + 2 : min(2 * c + 4, 6)]:
            copy.start()
        logits = dot(rt_ref[...], tokens[c], NT)
        lt_ref[c] = logits
        peak = jnp.max(logits, axis=1, keepdims=True)
        low = jnp.exp(logits - peak).astype(bf16).astype(f32)
        total = jnp.sum(low, axis=1, keepdims=True)
        raised = jnp.exp(logits - jnp.max(logits, axis=0, keepdims=True))
        combine = raised * (1.0 / jnp.sum(raised, axis=0, keepdims=True))
        low_up = pltpu.roll(low, 124, 0)
        combine_down = pltpu.roll(combine, 4, 0)
        own_in[c] = jnp.where(grad, 0.0, jnp.where(low_core, low, low_up)).astype(bf16)
        weights_in[c] = jnp.where(grad, 0.0, jnp.where(low_core, low_up, low)).astype(bf16)
        near = jnp.where(low_core, combine_down, combine)
        own_out[c] = jnp.where(grad, near, 0.0).astype(bf16)
        far = jnp.where(low_core, combine, combine_down)
        weights_out[c] = jnp.where(grad, far, 0.0).astype(bf16)
        at = STAT + 8 * c
        stats = jnp.where(lane == at, peak, jnp.where(lane == at + 3, total, stats))
    stats_up = pltpu.roll(stats, 124, 0)
    grad_row = is_grad_row((128, 128))
    ones = jnp.where((lane >= STAT) & (lane % 8 == 3), 1.0, 0.0)
    near = jnp.where(low_core, stats, stats_up)
    far = jnp.where(low_core, stats_up, stats)
    own_stats[...] = spread_triple(jnp.where(grad_row, ones, near))
    far = spread_triple(jnp.where(grad_row, ones, far))
    fill_parts(theirs, weights_in, weights_out, tokens, cot, far, copies[CLIPS:])


def own_body(core_ref, own_in, own_out, own_stats, tokens, cot, rt_ref, lt_ref, mine, rt_out, lt_out):
    fill_parts(mine, own_in, own_out, tokens, cot, own_stats[...])
    pick, _ = slot_of_row(core_ref[0])
    rt_out[...] = dot(pick.astype(f32).astype(bf16), rt_ref[...]).astype(bf16)
    low_core = core_ref[0] == 0
    grad = is_grad_row((128, TOK))
    for c in range(CLIPS):
        logits = lt_ref[c]
        low = jnp.where(grad, pltpu.roll(logits, 4, 0), logits)
        high = jnp.where(grad, logits, pltpu.roll(logits, 124, 0))
        lt_out[c, :128] = jnp.where(low_core, low, high)
        lt_out[c, 128:] = jnp.where(low_core, high, low)


def pair_body(a_ref, b_ref, out):
    columns, stats = merge_stats([x[0, :, :, 384:].astype(f32).reshape(128, 128) for x in (a_ref, b_ref)])
    for j in range(8):
        wide = [x[j].astype(f32).reshape(128, PART) for x in (a_ref, b_ref)]
        merged = merge_tiles(wide, columns, stats).astype(bf16)
        out[j] = merged[:64].reshape(8, 8, PART)
        out[8 + j] = merged[64:].reshape(8, 8, PART)


def members_body(x_ref, out):
    blocks = [x_ref[e].astype(f32).reshape(64, PART) for e in range(16)]
    out[...] = merge_blocks(blocks).reshape(8, 8, PART)


def owner_body(x_ref, out, own):
    merged = merge_blocks([x_ref[z] for z in range(8)])
    last = merged[:, 384:]
    joined = join_triple(last)
    grad = is_grad_row((8, 1))
    totals = [joined[:, STAT + 8 * c + 3 : STAT + 8 * c + 4] for c in range(CLIPS)]
    inverse = [jnp.where(grad, 1.0, 1.0 / total) for total in totals]
    lane = lanes_of(last.shape)
    tiles = [merged[:, 128 * c : 128 * c + 128] * inverse[c] for c in range(CLIPS)]
    tiles.append(jnp.where(lane < STAT, last * by_quarter(inverse, lane), last))
    rows = jnp.concatenate(tiles, axis=1)
    own[...] = rows
    low = rows.astype(bf16)
    for e in range(8):
        out[e] = low


def gelu_parts(v):
    t = jnp.tanh(GELU_C * (v + GELU_A * (v * v * v)))
    value = 0.5 * v * (1.0 + t)
    slope = 0.5 * (1.0 + t) + 0.5 * v * (1.0 - t * t) * (GELU_C * (1.0 + 3.0 * GELU_A * (v * v)))
    return value, slope


def expert_body(x_ref, w_in, w_out, out, stats_out):
    blocks = [x_ref[e].astype(f32) for e in range(8)]
    stats_out[...] = join_triple(blocks[0][:, 384:])
    low = jnp.concatenate([rows_of(blocks, c) for c in range(CLIPS)], axis=0).astype(bf16)
    row = lax.broadcasted_iota(jnp.int32, (ROWS, 640), 0)
    grad = row % 8 >= 4
    acc = jnp.zeros((ROWS, D), f32)
    for i in range(2):
        own = (row % 4) // 2 == i
        value, slope = gelu_parts(dot(low, w_in[i]))
        d_pre = dot(low, w_out[i], NT) * pltpu.roll(slope, 4, 0)
        hidden = jnp.where(own & jnp.logical_not(grad), value, 0.0).astype(bf16)
        d_pre = jnp.where(own & grad, d_pre, 0.0).astype(bf16)
        acc = acc + dot(hidden, w_out[i]) + dot(d_pre, w_in[i], NT)
    by_clip = [acc[8 * c : 8 * c + 8] for c in range(CLIPS)]
    tails = [rows[:, 1024:] for rows in by_clip]
    empty = jnp.zeros((8, 128), f32)
    for j in range(8):
        tiles = [rows[:, 128 * j : 128 * j + 128] for rows in by_clip]
        out[j] = jnp.concatenate(tiles + [last_tile(tails, j, empty)], axis=1)


def result_body(x_ref, joined, own, out):
    acc = x_ref[0]
    for e in range(1, 8):
        acc = acc + x_ref[e]
    low = acc.astype(bf16).astype(f32)
    products = low * pltpu.roll(own[...], 4, 0)
    lane = lanes_of((8, 128))
    grad = is_grad_row((8, 128))
    kept = jnp.where((lane % 8 == 0) | (lane % 8 == 3), joined[...], 0.0)
    dots = jnp.zeros((8, 128), f32)
    for c in range(CLIPS):
        both = products[:, 128 * c : 128 * c + 128]
        both = both + jnp.where(lane // 32 == c, products[:, 384:], 0.0)
        total = jnp.sum(both, axis=1, keepdims=True)
        dots = jnp.where(lane == STAT + 8 * c, total, dots)
    stats = spread_triple(jnp.where(lane < STAT, 0.0, jnp.where(grad, dots, kept)))
    last = jnp.where(lane < STAT, low[:, 384:], stats)
    full = jnp.concatenate([low[:, :384], last], axis=1).astype(bf16)
    for z in range(8):
        out[z] = full


def copies_body(x_ref, out):
    for e in range(16):
        out[e] = x_ref[...]


def half_of(g, tokens, cot, low_ref):
    blocks = [
        jnp.concatenate([g[8 * yl + j].astype(f32).reshape(64, PART) for yl in range(2)], axis=0)
        for j in range(8)
    ]
    dots = functools.reduce(jnp.add, [part[:, 384:] for part in blocks])
    d_combine, d_dispatch = [], []
    for c in range(CLIPS):
        low = rows_of(blocks, c).astype(bf16)
        low_ref[c] = low
        d_combine.append(dot(low, cot[c], NT))
        d_dispatch.append(dot(low, tokens[c], NT))
    return d_combine, d_dispatch, join_triple(dots), join_triple(blocks[0][:, 384:])


def near_body(tokens, cot, g, low_ref, dc_ref, dd_ref, dots_ref, stats_ref):
    d_combine, d_dispatch, dots, stats = half_of(g, tokens, cot, low_ref)
    for c in range(CLIPS):
        dc_ref[c] = d_combine[c]
        dd_ref[c] = d_dispatch[c]
    dots_ref[...] = dots
    stats_ref[...] = stats


def logit_body(
    tokens, cot, lt_ref, dc_ref, dd_ref, dots_ref, stats_ref, g,
    r_mine, r_theirs, dl_ref, w_ref, low_ref, r_sum,
):
    grad = is_grad_row((256, TOK))
    grad_half = is_grad_row((256, 640))
    far_combine, far_dispatch, far_dots, far_stats = half_of(g, tokens, cot, low_ref)
    dots = jnp.concatenate([dots_ref[...], far_dots], axis=0)
    stats = pltpu.roll(jnp.concatenate([stats_ref[...], far_stats], axis=0), 4, 0)
    for c in range(CLIPS):
        at = STAT + 8 * c
        peak = stats[:, at : at + 1]
        total = stats[:, at + 3 : at + 4]
        column_dot = dots[:, at : at + 1]
        logits = lt_ref[c]
        raised = jnp.exp(logits - jnp.max(logits, axis=0, keepdims=True))
        combine = raised * (2.0 / jnp.sum(raised, axis=0, keepdims=True))
        combine = jnp.where(grad, 0.0, combine)
        d_combine = jnp.concatenate([dc_ref[c], far_combine[c]], axis=0)
        inner = jnp.sum(combine * d_combine, axis=0, keepdims=True)
        dispatch = jnp.where(grad, jnp.exp(logits - peak) * (1.0 / total), 0.0)
        d_dispatch = jnp.concatenate([dd_ref[c], far_dispatch[c]], axis=0)
        own = jnp.where(grad, dispatch * (d_dispatch - column_dot), combine * (d_combine - inner))
        d_logit = (own + swap_halves(own, grad)).astype(bf16)
        part = dot(d_logit, tokens[c])
        part = jnp.where(grad_half, part[:, 640:], part[:, :640])
        if c == 0:
            r_sum[...] = part
        else:
            r_sum[...] += part
        dl_ref[c] = jnp.where(grad, 0.0, d_logit.astype(f32)).astype(bf16)
        w_ref[c] = dispatch.astype(bf16)
    r_mine[...] = r_sum[:128].astype(bf16).reshape(16, 8, 640)
    r_theirs[...] = r_sum[128:].astype(bf16).reshape(16, 8, 640)


def tokens_body(clips, dl_ref, w_ref, rt_ref, near_ref, far_ref, *rest):
    out, buffer, sems = rest[-3:]
    copies = []
    for c in clips:
        rows = jnp.concatenate([near_ref[c], far_ref[c]], axis=0)
        tile = dot(dl_ref[c], rt_ref[...], TN) + dot(w_ref[c], rows, TN)
        buffer[c] = tile.astype(bf16)
        copies.append(pltpu.make_async_copy(buffer.at[c], out.at[c], sems.at[c]))
        copies[-1].start()
    for copy in copies:
        copy.wait()


def token_clips(clips, *args):
    local = (CLIPS, TOK, D)
    return pl.pallas_call(
        functools.partial(tokens_body, clips),
        out_shape=jax.ShapeDtypeStruct(local, bf16),
        in_specs=[pl.BlockSpec(memory_space=pltpu.VMEM)] * 5
        + [pl.BlockSpec(memory_space=pltpu.HBM)] * (len(args) - 5),
        out_specs=pl.BlockSpec(memory_space=pltpu.HBM),
        scratch_shapes=[pltpu.VMEM(local, bf16), pltpu.SemaphoreType.DMA((CLIPS,))],
        input_output_aliases={5: 0} if len(args) > 5 else {},
        compiler_params=pltpu.CompilerParams(vmem_limit_bytes=16 * MiB),
        cost_estimate=pl.CostEstimate(flops=10**9, bytes_accessed=3 * 10**6, transcendentals=0),
    )(*args)


def add_body(a_ref, b_ref, out):
    out[...] = (a_ref[...].astype(f32) + b_ref[...].astype(f32)).astype(bf16)


def spread_body(x_ref, out):
    acc = x_ref[0].astype(f32)
    for i in range(1, x_ref.shape[0]):
        acc = acc + x_ref[i].astype(f32)
    acc = acc.astype(bf16)
    for i in range(out.shape[0]):
        out[i] = acc


def router_body(core_ref, mine, theirs, out):
    hit, t = slot_of_row(core_ref[0])
    rows = [x[...].astype(f32).reshape(128, 640) for x in (mine, theirs)]
    rows = jnp.concatenate(rows, axis=0).astype(bf16)
    for a in range(2):
        pick = (hit & ((t % 8) // 4 == a)).astype(f32).astype(bf16)
        out[a * 640 : (a + 1) * 640, :] = dot(rows, pick, TN)


def exchange(x, axes):
    return lax.all_to_all(x, axes, 0, 0, tiled=True)


def to_partner(x):
    return lax.ppermute(x, "core", [(0, 1), (1, 0)])


def per_device(tokens, router, w_in, w_out, cotangent):
    core = lax.axis_index("core").astype(jnp.int32).reshape(1)
    values = ((8, 16, 8, PART), bf16)
    planes = ((16, 8, 8, PART), bf16)
    local = (CLIPS, TOK, D)
    square = ((CLIPS, 256, TOK), bf16)
    own = ((CLIPS, 128, TOK), bf16)
    theirs, rt, lt, tokens, cotangent, own_in, own_out, own_stats = call(
        slots_body,
        [
            values,
            ((128, D), bf16),
            ((CLIPS, 128, TOK), f32),
            (local, bf16),
            (local, bf16),
            own,
            own,
            ((128, 128), f32),
        ],
        core,
        *[pltpu.with_memory_space_constraint(x, pltpu.HBM) for x in (router, tokens, cotangent)],
        scratch=[
            pltpu.VMEM((D, 128), bf16),
            pltpu.VMEM(*own),
            pltpu.VMEM(*own),
            pltpu.SemaphoreType.DMA((2, CLIPS)),
            pltpu.SemaphoreType.DMA,
        ],
        smem=(0,),
        hbm=(1, 2, 3),
        flops=3 * 10**9,
        nbytes=8 * 10**6,
        limit=24,
    )
    mine, rt, lt = call(
        own_body,
        [(values[0], f32), ((256, D), bf16), ((CLIPS, 256, TOK), f32)],
        core,
        own_in,
        own_out,
        own_stats,
        tokens,
        cotangent,
        rt,
        lt,
        smem=(0,),
        flops=10**9,
        nbytes=8 * 10**6,
        limit=24,
    )
    (sums,) = call(pair_body, [planes], mine, to_partner(theirs), flops=10**10, nbytes=3 * 10**6)
    (sums,) = call(
        members_body, [((8, 8, PART), f32)], exchange(sums, PLANE), flops=10**10, nbytes=10**6
    )
    sums, own = call(
        owner_body,
        [((8, 8, PART), bf16), ((8, PART), f32)],
        exchange(sums, ("z",)),
        nbytes=10**5,
    )
    parts, stats = call(
        expert_body,
        [((8, 8, PART), f32), ((8, 128), f32)],
        exchange(sums, EXP),
        w_in,
        w_out,
        flops=10**9,
        nbytes=8 * 10**6,
    )
    (result,) = call(
        result_body, [((8, 8, PART), bf16)], exchange(parts, EXP), stats, own, nbytes=10**5
    )
    (result,) = call(copies_body, [planes], exchange(result, ("z",)), nbytes=10**6)
    g_mine = exchange(result, PLANE)
    g_theirs = to_partner(g_mine)
    half = ((16, 8, 640), bf16)
    pair = ((CLIPS, 128, TOK), f32)
    near, d_combine, d_dispatch, dots, stats = call(
        near_body,
        [((CLIPS, 128, D), bf16), pair, pair, ((128, 128), f32), ((128, 128), f32)],
        tokens,
        cotangent,
        g_mine,
        flops=10**9,
        nbytes=6 * 10**6,
    )
    r_mine, r_theirs, d_logit, dispatch, far = call(
        logit_body,
        [half, half, square, square, ((CLIPS, 128, D), bf16)],
        tokens,
        cotangent,
        lt,
        d_combine,
        d_dispatch,
        dots,
        stats,
        g_theirs,
        scratch=[pltpu.VMEM((256, 640), f32)],
        flops=3 * 10**9,
        nbytes=10**7,
        limit=24,
    )
    work = (d_logit, dispatch, rt, near, far)
    got, d_tokens = lax.optimization_barrier((to_partner(r_theirs), token_clips((0,), *work)))
    (r_mine,) = call(add_body, [half], r_mine, got, nbytes=10**6)
    d_tokens = token_clips((1, 2), *work, d_tokens)
    r_mine = exchange(r_mine, PLANE)
    (r_mine,) = call(spread_body, [((8, 8, 640), bf16)], r_mine, nbytes=10**5)
    r_mine = exchange(r_mine, ("z",))
    (r_mine,) = call(spread_body, [half], r_mine, nbytes=10**5)
    r_mine = exchange(r_mine, PLANE)
    (d_router,) = call(
        router_body, [((D, 128), f32)], core, r_mine, to_partner(r_mine), smem=(0,), nbytes=2 * 10**6
    )
    return (d_tokens, d_router)


def solution(mesh):
    fine = Mesh(mesh.devices.reshape(tuple(SIZES.values())), AXES)
    seq = ("yl", "z", "core")
    placed = (
        P(None, AXES, None),
        P(),
        P(seq, None, EXP),
        P(seq, EXP, None),
        P(None, AXES, None),
    )
    return jax.shard_map(
        per_device,
        mesh=fine,
        in_specs=placed,
        out_specs=(P(None, AXES, None), P()),
        check_vma=False,
    )
```

```python
import functools

import jax
import jax.numpy as jnp
from jax import lax
from jax.experimental import pallas as pl
from jax.experimental.pallas import tpu as pltpu
from jax.sharding import Mesh, PartitionSpec as P

SIZES = {"yl": 2, "z": 8, "core": 2, "yh": 2, "x": 4}
AXES = tuple(SIZES)
EXP = ("yh", "x")
PLANE = ("yl", "yh", "x")

D = 1280
CLIPS = 3
TOK = 256
ROWS = 24
PART = 512
STAT = 96
MiB = 1024 * 1024
GELU_C = 0.7978845608028654
GELU_A = 0.044715

bf16 = jnp.bfloat16
f32 = jnp.float32

NT = (((1,), (1,)), ((), ()))
TN = (((0,), (0,)), ((), ()))


def dot(a, b, dims=None):
    if dims is None:
        return jnp.dot(a, b, preferred_element_type=f32)
    return lax.dot_general(a, b, dims, preferred_element_type=f32)


def is_grad_row(shape):
    return lax.broadcasted_iota(jnp.int32, shape, 0) % 8 >= 4


def swap_halves(v, grad):
    n = v.shape[0]
    return jnp.where(grad, pltpu.roll(v, 4, 0), pltpu.roll(v, n - 4, 0))


def lanes_of(shape):
    return lax.broadcasted_iota(jnp.int32, shape, len(shape) - 1)


def split(value):
    high = value.astype(bf16).astype(f32)
    rest = value - high
    middle = rest.astype(bf16).astype(f32)
    return high, middle, rest - middle


def spread_triple(value):
    high, middle, low = split(value)
    return high + pltpu.roll(middle, 1, 1) + pltpu.roll(low, 2, 1)


def join_triple(stats):
    return stats + pltpu.roll(stats, 127, 1) + pltpu.roll(stats, 126, 1)


def clip_columns(x):
    return [x[:, STAT + 8 * c : STAT + 8 * c + 1] for c in range(CLIPS)]


def by_quarter(columns, lane):
    first = jnp.where(lane < 32, columns[0], columns[1])
    return jnp.where(lane < 64, first, columns[2])


def merge_stats(last):
    joined = [join_triple(x) for x in last]
    peak = functools.reduce(jnp.maximum, joined)
    scales = [jnp.exp(jnp.minimum(j - peak, 0.0)) for j in joined]
    total = functools.reduce(jnp.add, [pltpu.roll(x, 3, 1) * j for x, j in zip(scales, joined)])
    lane = lanes_of(peak.shape)
    stats = jnp.where(lane % 8 == 0, peak, jnp.where(lane % 8 == 3, total, 0.0))
    stats = spread_triple(jnp.where(lane < STAT, 0.0, stats))
    return [clip_columns(x) for x in scales], stats


def merge_tiles(wide, columns, stats):
    tiles = []
    for c in range(CLIPS):
        lanes = slice(128 * c, 128 * c + 128)
        parts = [col[c] * b[:, lanes] for b, col in zip(wide, columns)]
        tiles.append(functools.reduce(jnp.add, parts))
    lane = lanes_of(stats.shape)
    parts = [by_quarter(col, lane) * b[:, 384:] for b, col in zip(wide, columns)]
    tiles.append(jnp.where(lane < STAT, functools.reduce(jnp.add, parts), stats))
    return jnp.concatenate(tiles, axis=1)


def merge_blocks(blocks):
    wide = [b.astype(f32) for b in blocks]
    return merge_tiles(wide, *merge_stats([b[:, 384:] for b in wide]))


def rows_of(blocks, c):
    lane = lanes_of((blocks[0].shape[0], 128))
    tiles = [b[:, 128 * c : 128 * c + 128] for b in blocks]
    for first in (0, 4):
        tile = None
        for q in range(4):
            turned = blocks[first + q][:, 384:]
            if q != c:
                turned = pltpu.roll(turned, 32 * (q - c) % 128, 1)
            tile = turned if tile is None else jnp.where(lane // 32 == q, turned, tile)
        tiles.append(tile)
    return jnp.concatenate(tiles, axis=1)


def last_tile(tails, j, stats):
    lane = lanes_of(stats.shape)
    out = stats
    for c, tail in enumerate(tails):
        tile = tail[:, 128 * (j // 4) : 128 * (j // 4) + 128]
        if j % 4 != c:
            tile = pltpu.roll(tile, 32 * (c - j % 4) % 128, 1)
        out = jnp.where(lane // 32 == c, tile, out)
    return out


def call(body, outs, *args, scratch=(), flops=0, nbytes=0, smem=(), hbm=(), limit=16):
    spaces = [
        pltpu.SMEM if i in smem else pltpu.HBM if i in hbm else pltpu.VMEM for i in range(len(args))
    ]
    return pl.pallas_call(
        body,
        out_shape=[jax.ShapeDtypeStruct(s, t) for s, t in outs],
        in_specs=[pl.BlockSpec(memory_space=s) for s in spaces],
        out_specs=[pl.BlockSpec(memory_space=pltpu.VMEM) for _ in outs],
        scratch_shapes=list(scratch),
        compiler_params=pltpu.CompilerParams(vmem_limit_bytes=limit * MiB),
        cost_estimate=pl.CostEstimate(flops=flops, bytes_accessed=nbytes, transcendentals=0),
    )(*args)


def slot_of_row(core):
    t = lax.broadcasted_iota(jnp.int32, (256, 128), 0)
    s = lax.broadcasted_iota(jnp.int32, (256, 128), 1)
    half = t // 128
    slot = 8 * ((t % 128) // 8) + 4 * (half + core * (1 - 2 * half)) + t % 4
    return s == slot, t


def fill_parts(out, weights_in, weights_out, tokens, cot, stats, before=None):
    def product(c, lanes):
        return dot(weights_in[c], tokens[c, :, lanes]) + dot(weights_out[c], cot[c, :, lanes])

    for c in range(CLIPS):
        if before is not None:
            before[c].wait()
        for i in range(4):
            part = product(c, slice(256 * i, 256 * i + 256)).reshape(16, 8, 256)
            for h in range(2):
                tile = part[:, :, 128 * h : 128 * h + 128]
                out[2 * i + h, :, :, 128 * c : 128 * c + 128] = tile.astype(out.dtype)
    tails = [product(c, slice(1024, 1280)) for c in range(CLIPS)]
    for j in range(8):
        out[j, :, :, 384:] = last_tile(tails, j, stats).reshape(16, 8, 128).astype(out.dtype)


def slots_body(
    core_ref, router_hbm, tokens_hbm, cot_hbm, theirs, rt_ref, lt_ref, tokens, cot,
    own_in, own_out, own_stats, router, weights_in, weights_out, sems, router_sem,
):
    first = pltpu.make_async_copy(router_hbm, router, router_sem)
    copies = [
        pltpu.make_async_copy(src.at[c], dst.at[c], sems.at[i, c])
        for i, (src, dst) in enumerate(((tokens_hbm, tokens), (cot_hbm, cot)))
        for c in range(CLIPS)
    ]
    first.start()
    for copy in copies:
        copy.start()
    row = lax.broadcasted_iota(jnp.int32, (128, 128), 0)
    lane = lanes_of((128, 128))
    same = (row == lane).astype(f32).astype(bf16)
    first.wait()
    rt_ref[...] = dot(same, router[...], NT).astype(bf16)
    low_core = core_ref[0] == 0
    grad = is_grad_row((128, TOK))
    stats = jnp.zeros((128, 128), f32)
    for c in range(CLIPS):
        copies[c].wait()
        logits = dot(rt_ref[...], tokens[c], NT)
        lt_ref[c] = logits
        peak = jnp.max(logits, axis=1, keepdims=True)
        low = jnp.exp(logits - peak).astype(bf16).astype(f32)
        total = jnp.sum(low, axis=1, keepdims=True)
        raised = jnp.exp(logits - jnp.max(logits, axis=0, keepdims=True))
        combine = raised * (1.0 / jnp.sum(raised, axis=0, keepdims=True))
        low_up = pltpu.roll(low, 124, 0)
        combine_down = pltpu.roll(combine, 4, 0)
        own_in[c] = jnp.where(grad, 0.0, jnp.where(low_core, low, low_up)).astype(bf16)
        weights_in[c] = jnp.where(grad, 0.0, jnp.where(low_core, low_up, low)).astype(bf16)
        near = jnp.where(low_core, combine_down, combine)
        own_out[c] = jnp.where(grad, near, 0.0).astype(bf16)
        far = jnp.where(low_core, combine, combine_down)
        weights_out[c] = jnp.where(grad, far, 0.0).astype(bf16)
        at = STAT + 8 * c
        stats = jnp.where(lane == at, peak, jnp.where(lane == at + 3, total, stats))
    stats_up = pltpu.roll(stats, 124, 0)
    grad_row = is_grad_row((128, 128))
    ones = jnp.where((lane >= STAT) & (lane % 8 == 3), 1.0, 0.0)
    near = jnp.where(low_core, stats, stats_up)
    far = jnp.where(low_core, stats_up, stats)
    own_stats[...] = spread_triple(jnp.where(grad_row, ones, near))
    far = spread_triple(jnp.where(grad_row, ones, far))
    fill_parts(theirs, weights_in, weights_out, tokens, cot, far, copies[CLIPS:])


def own_body(core_ref, own_in, own_out, own_stats, tokens, cot, rt_ref, lt_ref, mine, rt_out, lt_out):
    fill_parts(mine, own_in, own_out, tokens, cot, own_stats[...])
    pick, _ = slot_of_row(core_ref[0])
    rt_out[...] = dot(pick.astype(f32).astype(bf16), rt_ref[...]).astype(bf16)
    low_core = core_ref[0] == 0
    grad = is_grad_row((128, TOK))
    for c in range(CLIPS):
        logits = lt_ref[c]
        low = jnp.where(grad, pltpu.roll(logits, 4, 0), logits)
        high = jnp.where(grad, logits, pltpu.roll(logits, 124, 0))
        lt_out[c, :128] = jnp.where(low_core, low, high)
        lt_out[c, 128:] = jnp.where(low_core, high, low)


def pair_body(a_ref, b_ref, out):
    columns, stats = merge_stats([x[0, :, :, 384:].astype(f32).reshape(128, 128) for x in (a_ref, b_ref)])
    for j in range(8):
        wide = [x[j].astype(f32).reshape(128, PART) for x in (a_ref, b_ref)]
        merged = merge_tiles(wide, columns, stats).astype(bf16)
        out[j] = merged[:64].reshape(8, 8, PART)
        out[8 + j] = merged[64:].reshape(8, 8, PART)


def members_body(x_ref, out):
    blocks = [x_ref[e].astype(f32).reshape(64, PART) for e in range(16)]
    out[...] = merge_blocks(blocks).reshape(8, 8, PART)


def owner_body(x_ref, out, own):
    merged = merge_blocks([x_ref[z] for z in range(8)])
    last = merged[:, 384:]
    joined = join_triple(last)
    grad = is_grad_row((8, 1))
    totals = [joined[:, STAT + 8 * c + 3 : STAT + 8 * c + 4] for c in range(CLIPS)]
    inverse = [jnp.where(grad, 1.0, 1.0 / total) for total in totals]
    lane = lanes_of(last.shape)
    tiles = [merged[:, 128 * c : 128 * c + 128] * inverse[c] for c in range(CLIPS)]
    tiles.append(jnp.where(lane < STAT, last * by_quarter(inverse, lane), last))
    rows = jnp.concatenate(tiles, axis=1)
    own[...] = rows
    low = rows.astype(bf16)
    for e in range(8):
        out[e] = low


def gelu_parts(v):
    t = jnp.tanh(GELU_C * (v + GELU_A * (v * v * v)))
    value = 0.5 * v * (1.0 + t)
    slope = 0.5 * (1.0 + t) + 0.5 * v * (1.0 - t * t) * (GELU_C * (1.0 + 3.0 * GELU_A * (v * v)))
    return value, slope


def expert_body(x_ref, w_in, w_out, out, stats_out):
    blocks = [x_ref[e].astype(f32) for e in range(8)]
    stats_out[...] = join_triple(blocks[0][:, 384:])
    low = jnp.concatenate([rows_of(blocks, c) for c in range(CLIPS)], axis=0).astype(bf16)
    row = lax.broadcasted_iota(jnp.int32, (ROWS, 640), 0)
    grad = row % 8 >= 4
    acc = jnp.zeros((ROWS, D), f32)
    for i in range(2):
        own = (row % 4) // 2 == i
        value, slope = gelu_parts(dot(low, w_in[i]))
        d_pre = dot(low, w_out[i], NT) * pltpu.roll(slope, 4, 0)
        hidden = jnp.where(own & jnp.logical_not(grad), value, 0.0).astype(bf16)
        d_pre = jnp.where(own & grad, d_pre, 0.0).astype(bf16)
        acc = acc + dot(hidden, w_out[i]) + dot(d_pre, w_in[i], NT)
    by_clip = [acc[8 * c : 8 * c + 8] for c in range(CLIPS)]
    tails = [rows[:, 1024:] for rows in by_clip]
    empty = jnp.zeros((8, 128), f32)
    for j in range(8):
        tiles = [rows[:, 128 * j : 128 * j + 128] for rows in by_clip]
        out[j] = jnp.concatenate(tiles + [last_tile(tails, j, empty)], axis=1)


def result_body(x_ref, joined, own, out):
    acc = x_ref[0]
    for e in range(1, 8):
        acc = acc + x_ref[e]
    low = acc.astype(bf16).astype(f32)
    products = low * pltpu.roll(own[...], 4, 0)
    lane = lanes_of((8, 128))
    grad = is_grad_row((8, 128))
    kept = jnp.where((lane % 8 == 0) | (lane % 8 == 3), joined[...], 0.0)
    dots = jnp.zeros((8, 128), f32)
    for c in range(CLIPS):
        both = products[:, 128 * c : 128 * c + 128]
        both = both + jnp.where(lane // 32 == c, products[:, 384:], 0.0)
        total = jnp.sum(both, axis=1, keepdims=True)
        dots = jnp.where(lane == STAT + 8 * c, total, dots)
    stats = spread_triple(jnp.where(lane < STAT, 0.0, jnp.where(grad, dots, kept)))
    last = jnp.where(lane < STAT, low[:, 384:], stats)
    full = jnp.concatenate([low[:, :384], last], axis=1).astype(bf16)
    for z in range(8):
        out[z] = full


def copies_body(x_ref, out):
    for e in range(16):
        out[e] = x_ref[...]


def half_of(g, tokens, cot, low_ref):
    blocks = [
        jnp.concatenate([g[8 * yl + j].astype(f32).reshape(64, PART) for yl in range(2)], axis=0)
        for j in range(8)
    ]
    dots = functools.reduce(jnp.add, [part[:, 384:] for part in blocks])
    d_combine, d_dispatch = [], []
    for c in range(CLIPS):
        low = rows_of(blocks, c).astype(bf16)
        low_ref[c] = low
        d_combine.append(dot(low, cot[c], NT))
        d_dispatch.append(dot(low, tokens[c], NT))
    return d_combine, d_dispatch, join_triple(dots), join_triple(blocks[0][:, 384:])


def near_body(tokens, cot, g, low_ref, dc_ref, dd_ref, dots_ref, stats_ref):
    d_combine, d_dispatch, dots, stats = half_of(g, tokens, cot, low_ref)
    for c in range(CLIPS):
        dc_ref[c] = d_combine[c]
        dd_ref[c] = d_dispatch[c]
    dots_ref[...] = dots
    stats_ref[...] = stats


def logit_body(
    tokens, cot, lt_ref, dc_ref, dd_ref, dots_ref, stats_ref, g,
    r_mine, r_theirs, dl_ref, w_ref, low_ref, r_sum,
):
    grad = is_grad_row((256, TOK))
    grad_half = is_grad_row((256, 640))
    far_combine, far_dispatch, far_dots, far_stats = half_of(g, tokens, cot, low_ref)
    dots = jnp.concatenate([dots_ref[...], far_dots], axis=0)
    stats = pltpu.roll(jnp.concatenate([stats_ref[...], far_stats], axis=0), 4, 0)
    for c in range(CLIPS):
        at = STAT + 8 * c
        peak = stats[:, at : at + 1]
        total = stats[:, at + 3 : at + 4]
        column_dot = dots[:, at : at + 1]
        logits = lt_ref[c]
        raised = jnp.exp(logits - jnp.max(logits, axis=0, keepdims=True))
        combine = raised * (2.0 / jnp.sum(raised, axis=0, keepdims=True))
        combine = jnp.where(grad, 0.0, combine)
        d_combine = jnp.concatenate([dc_ref[c], far_combine[c]], axis=0)
        inner = jnp.sum(combine * d_combine, axis=0, keepdims=True)
        dispatch = jnp.where(grad, jnp.exp(logits - peak) * (1.0 / total), 0.0)
        d_dispatch = jnp.concatenate([dd_ref[c], far_dispatch[c]], axis=0)
        own = jnp.where(grad, dispatch * (d_dispatch - column_dot), combine * (d_combine - inner))
        d_logit = (own + swap_halves(own, grad)).astype(bf16)
        part = dot(d_logit, tokens[c])
        part = jnp.where(grad_half, part[:, 640:], part[:, :640])
        if c == 0:
            r_sum[...] = part
        else:
            r_sum[...] += part
        dl_ref[c] = jnp.where(grad, 0.0, d_logit.astype(f32)).astype(bf16)
        w_ref[c] = dispatch.astype(bf16)
    r_mine[...] = r_sum[:128].astype(bf16).reshape(16, 8, 640)
    r_theirs[...] = r_sum[128:].astype(bf16).reshape(16, 8, 640)


def tokens_body(clips, dl_ref, w_ref, rt_ref, near_ref, far_ref, *rest):
    out, buffer, sems = rest[-3:]
    copies = []
    for c in clips:
        rows = jnp.concatenate([near_ref[c], far_ref[c]], axis=0)
        tile = dot(dl_ref[c], rt_ref[...], TN) + dot(w_ref[c], rows, TN)
        buffer[c] = tile.astype(bf16)
        copies.append(pltpu.make_async_copy(buffer.at[c], out.at[c], sems.at[c]))
        copies[-1].start()
    for copy in copies:
        copy.wait()


def token_clips(clips, *args):
    local = (CLIPS, TOK, D)
    return pl.pallas_call(
        functools.partial(tokens_body, clips),
        out_shape=jax.ShapeDtypeStruct(local, bf16),
        in_specs=[pl.BlockSpec(memory_space=pltpu.VMEM)] * 5
        + [pl.BlockSpec(memory_space=pltpu.HBM)] * (len(args) - 5),
        out_specs=pl.BlockSpec(memory_space=pltpu.HBM),
        scratch_shapes=[pltpu.VMEM(local, bf16), pltpu.SemaphoreType.DMA((CLIPS,))],
        input_output_aliases={5: 0} if len(args) > 5 else {},
        compiler_params=pltpu.CompilerParams(vmem_limit_bytes=16 * MiB),
        cost_estimate=pl.CostEstimate(flops=10**9, bytes_accessed=3 * 10**6, transcendentals=0),
    )(*args)


def add_body(a_ref, b_ref, out):
    out[...] = (a_ref[...].astype(f32) + b_ref[...].astype(f32)).astype(bf16)


def spread_body(x_ref, out):
    acc = x_ref[0].astype(f32)
    for i in range(1, x_ref.shape[0]):
        acc = acc + x_ref[i].astype(f32)
    acc = acc.astype(bf16)
    for i in range(out.shape[0]):
        out[i] = acc


def router_body(core_ref, mine, theirs, out):
    hit, t = slot_of_row(core_ref[0])
    rows = [x[...].astype(f32).reshape(128, 640) for x in (mine, theirs)]
    rows = jnp.concatenate(rows, axis=0).astype(bf16)
    for a in range(2):
        pick = (hit & ((t % 8) // 4 == a)).astype(f32).astype(bf16)
        out[a * 640 : (a + 1) * 640, :] = dot(rows, pick, TN)


def exchange(x, axes):
    return lax.all_to_all(x, axes, 0, 0, tiled=True)


def to_partner(x):
    return lax.ppermute(x, "core", [(0, 1), (1, 0)])


def per_device(tokens, router, w_in, w_out, cotangent):
    core = lax.axis_index("core").astype(jnp.int32).reshape(1)
    values = ((8, 16, 8, PART), bf16)
    planes = ((16, 8, 8, PART), bf16)
    local = (CLIPS, TOK, D)
    square = ((CLIPS, 256, TOK), bf16)
    own = ((CLIPS, 128, TOK), bf16)
    theirs, rt, lt, tokens, cotangent, own_in, own_out, own_stats = call(
        slots_body,
        [
            values,
            ((128, D), bf16),
            ((CLIPS, 128, TOK), f32),
            (local, bf16),
            (local, bf16),
            own,
            own,
            ((128, 128), f32),
        ],
        core,
        *[pltpu.with_memory_space_constraint(x, pltpu.HBM) for x in (router, tokens, cotangent)],
        scratch=[
            pltpu.VMEM((D, 128), bf16),
            pltpu.VMEM(*own),
            pltpu.VMEM(*own),
            pltpu.SemaphoreType.DMA((2, CLIPS)),
            pltpu.SemaphoreType.DMA,
        ],
        smem=(0,),
        hbm=(1, 2, 3),
        flops=3 * 10**9,
        nbytes=8 * 10**6,
        limit=24,
    )
    mine, rt, lt = call(
        own_body,
        [(values[0], f32), ((256, D), bf16), ((CLIPS, 256, TOK), f32)],
        core,
        own_in,
        own_out,
        own_stats,
        tokens,
        cotangent,
        rt,
        lt,
        smem=(0,),
        flops=10**9,
        nbytes=8 * 10**6,
        limit=24,
    )
    (sums,) = call(pair_body, [planes], mine, to_partner(theirs), flops=10**10, nbytes=3 * 10**6)
    (sums,) = call(
        members_body, [((8, 8, PART), f32)], exchange(sums, PLANE), flops=10**10, nbytes=10**6
    )
    sums, own = call(
        owner_body,
        [((8, 8, PART), bf16), ((8, PART), f32)],
        exchange(sums, ("z",)),
        nbytes=10**5,
    )
    parts, stats = call(
        expert_body,
        [((8, 8, PART), f32), ((8, 128), f32)],
        exchange(sums, EXP),
        w_in,
        w_out,
        flops=10**9,
        nbytes=8 * 10**6,
    )
    (result,) = call(
        result_body, [((8, 8, PART), bf16)], exchange(parts, EXP), stats, own, nbytes=10**5
    )
    (result,) = call(copies_body, [planes], exchange(result, ("z",)), nbytes=10**6)
    g_mine = exchange(result, PLANE)
    g_theirs = to_partner(g_mine)
    half = ((16, 8, 640), bf16)
    pair = ((CLIPS, 128, TOK), f32)
    near, d_combine, d_dispatch, dots, stats = call(
        near_body,
        [((CLIPS, 128, D), bf16), pair, pair, ((128, 128), f32), ((128, 128), f32)],
        tokens,
        cotangent,
        g_mine,
        flops=10**9,
        nbytes=6 * 10**6,
    )
    r_mine, r_theirs, d_logit, dispatch, far = call(
        logit_body,
        [half, half, square, square, ((CLIPS, 128, D), bf16)],
        tokens,
        cotangent,
        lt,
        d_combine,
        d_dispatch,
        dots,
        stats,
        g_theirs,
        scratch=[pltpu.VMEM((256, 640), f32)],
        flops=3 * 10**9,
        nbytes=10**7,
        limit=24,
    )
    work = (d_logit, dispatch, rt, near, far)
    got, d_tokens = lax.optimization_barrier((to_partner(r_theirs), token_clips((0,), *work)))
    (r_mine,) = call(add_body, [half], r_mine, got, nbytes=10**6)
    d_tokens = token_clips((1, 2), *work, d_tokens)
    r_mine = exchange(r_mine, PLANE)
    (r_mine,) = call(spread_body, [((8, 8, 640), bf16)], r_mine, nbytes=10**5)
    r_mine = exchange(r_mine, ("z",))
    (r_mine,) = call(spread_body, [half], r_mine, nbytes=10**5)
    r_mine = exchange(r_mine, PLANE)
    (d_router,) = call(
        router_body, [((D, 128), f32)], core, r_mine, to_partner(r_mine), smem=(0,), nbytes=2 * 10**6
    )
    return (d_tokens, d_router)


def solution(mesh):
    fine = Mesh(mesh.devices.reshape(tuple(SIZES.values())), AXES)
    seq = ("yl", "z", "core")
    placed = (
        P(None, AXES, None),
        P(),
        P(seq, None, EXP),
        P(seq, EXP, None),
        P(None, AXES, None),
    )
    return jax.shard_map(
        per_device,
        mesh=fine,
        in_specs=placed,
        out_specs=(P(None, AXES, None), P()),
        check_vma=False,
    )
```
